32 devices in a mesh: din: 4 (over z), dout: 8 (over y, x, core).
Axes of the slice: x: 2, y: 2, z: 4, core: 2. Of those that a mesh axis runs over, the one named last changes fastest.
Arguments:
- inputs: bfloat16 [2048, 8192], P('dout', 'din'), may hold values from -6 to 6
- cotangent: bfloat16 [2048, 28672], P('din', 'dout'), may hold values from -6 to 6
- codes: int32 [2, 1024, 28672], P(None, 'din', 'dout'), may hold values from 0 to 255
- codebooks: float32 [2, 256, 8], replicated, may hold values from -6 to 6
- scales: float32 [28672], P('dout'), may hold values from 0.5 to 2
- book_mean: float32 [2, 256, 8], replicated, may hold values from -3 to 3
- book_var: float32 [2, 256, 8], replicated, may hold values from 0.1 to 1
- scale_mean: float32 [28672], P('dout'), may hold values from -3 to 3
- scale_var: float32 [28672], P('dout'), may hold values from 0.1 to 1
Outputs:
- grad_input: bfloat16 [2048, 8192], P('dout', 'din')
- book_grad: float32 [2, 256, 8], replicated
- new_books: float32 [2, 256, 8], replicated
- new_book_mean: float32 [2, 256, 8], replicated
- new_book_var: float32 [2, 256, 8], replicated
- new_scales: float32 [28672], P('dout')
- new_scale_mean: float32 [28672], P('dout')
- new_scale_var: float32 [28672], P('dout')
The draws below stay inside these ranges and needn't reach their ends.
Inputs may be any that keep to these rules, and one draw needn't show every extreme that they name: codes[b, g, o] names the entry of codebook b used for input features 8 * g to 8 * g + 7 of output o.
All inputs are finite; a program needn't handle non-finite values.
Results may differ from the reference program's by a relative error of at most 0.0057.
Values may be sent and summed in bfloat16 or wider, within the bound.
No kernel may reach another device: no remote copies, remote signals or barrier semaphores. Data moves between devices by JAX's collectives and lax.ppermute only.
A program may use at most 128 MiB of HBM per device.

```python
import math
import jax
import jax.numpy as jnp
from jax import lax

DIN = 8192
DOUT = 28672
KCODE = 256
BOOKS = 2
GROUP = 8
TOKENS = 2048
N_DOUT = 8


def touch_ends(drawn, own_key, least, largest):
    longest = drawn.shape.index(max(drawn.shape))
    spots = []
    for shift in (0, 1):
        where = [jax.random.randint(jax.random.fold_in(own_key, axis), (), 0, length) for axis, length in enumerate(drawn.shape)]
        where[longest] = (where[longest] + shift) % drawn.shape[longest]
        spots.append(tuple(where))
    return drawn.at[spots[0]].set(least).at[spots[1]].set(largest)


def shard_levels(rng, shape, pieces, low, top_value):
    level, own = 1.0, jax.random.fold_in(rng, 6)
    for dim, shards_of in pieces:
        draws = jnp.exp(jax.random.uniform(jax.random.fold_in(own, dim), (shards_of,), jnp.float32, low / len(pieces), top_value / len(pieces)))
        level = level * jnp.repeat(draws, shape[dim] // shards_of).reshape([-1 if axis == dim else 1 for axis in range(len(shape))])
    return level


def noise(stream_key, extent, deviation, limit, shards=(), kind=jnp.bfloat16):
    entries = jax.random.normal(stream_key, extent, jnp.float32) * deviation
    if len(shards) > 0:
        entries = shard_levels(stream_key, extent, shards, -0.22, 0.18) * entries
    return jnp.clip(entries, min=-limit, max=limit).astype(kind)


def setup_inputs(seed: int = 0) -> dict:
    key_of = jax.random.split(jax.random.key(seed), 10)
    inputs = noise(key_of[0], (TOKENS, DIN), 1.0, 6.0, ((0, 8), (1, 4)))
    cotangent = noise(key_of[1], (TOKENS, DOUT), 1.0, 6.0, ((0, 4), (1, 8)))
    codes = touch_ends(jax.random.randint(key_of[2], (BOOKS, DIN // GROUP, DOUT), 0, KCODE), jax.random.fold_in(key_of[2], 1), 0, KCODE - 1).astype(jnp.int32)
    codebooks = noise(key_of[3], (BOOKS, KCODE, GROUP), 1.0, 6.0, (), jnp.float32)
    scales = jnp.clip(jnp.exp(math.log(2.0) - 1.3862944 * jax.random.uniform(key_of[4], (DOUT,), jnp.float32) ** shard_levels(key_of[4], (DOUT,), ((0, 8),), -0.2, 0.2)), 0.5, 2.0)
    book_mean = noise(key_of[5], (BOOKS, KCODE, GROUP), 0.5, 3.0, (), jnp.float32)
    book_var = jnp.clip(jnp.exp(jax.random.uniform(key_of[6], (BOOKS, KCODE, GROUP), jnp.float32, math.log(0.1), math.log(1.0))), 0.1, 1.0)
    scale_mean = noise(key_of[7], (DOUT,), 0.5, 3.0, ((0, 8),), jnp.float32)
    scale_var = jnp.clip(jnp.exp(math.log(1.0) - 2.3025851 * jax.random.uniform(key_of[8], (DOUT,), jnp.float32) ** shard_levels(key_of[8], (DOUT,), ((0, 8),), -0.2, 0.2)), 0.1, 1.0)
    return {"inputs": inputs, "cotangent": cotangent, "codes": codes, "codebooks": codebooks, "scales": scales, "book_mean": book_mean, "book_var": book_var, "scale_mean": scale_mean, "scale_var": scale_var}


beta_one = 0.9
beta_two = 0.999
adam_rate = 0.01
adam_eps = 1e-08
corr_one = 1.0 - 0.9 ** 10
corr_two = 1.0 - 0.999 ** 10

def adam_step(param, mean_old, var_old, gradient):
    mean_new = beta_one * mean_old + (1.0 - beta_one) * gradient
    var_new = beta_two * var_old + (1.0 - beta_two) * gradient * gradient
    update = mean_new / corr_one / (jnp.sqrt(var_new / corr_two) + adam_eps)
    return (param - adam_rate * update, mean_new, var_new)

def reference(inputs, cotangent, codes, codebooks, scales, book_mean, book_var, scale_mean, scale_var):
    norm_factor = 1.0 / (2.0 * DOUT) ** 0.5
    loss_scale = (TOKENS * DIN / 4096.0) ** 0.5
    coef = scales * norm_factor
    rounded = lax.optimization_barrier(codebooks.astype(jnp.bfloat16)).astype(jnp.float32)
    width = DOUT // N_DOUT
    groups = DIN // GROUP

    def block_step(state_tuple, block_index):
        gx_total, grad_total = state_tuple
        first_col = block_index * width
        code_block = lax.dynamic_slice_in_dim(codes, first_col, width, 2)
        coef_block = lax.dynamic_slice_in_dim(coef, first_col, width, 0)
        gy_block = lax.dynamic_slice_in_dim(cotangent, first_col, width, 1)
        decoded = rounded[0][code_block[0]] + rounded[1][code_block[1]]
        decoded = decoded.transpose(0, 2, 1).reshape(DIN, width)
        weights = (decoded * coef_block).astype(jnp.bfloat16)
        grad_w = jnp.dot(inputs.T, gy_block, preferred_element_type=jnp.float32)
        gx_total = gx_total + jnp.dot(gy_block, weights.T, preferred_element_type=jnp.float32)
        scaled = lax.optimization_barrier((grad_w * coef_block).astype(jnp.bfloat16)).astype(jnp.float32)
        flattened = scaled.reshape(groups, GROUP, width).transpose(0, 2, 1).reshape(-1, GROUP)
        book_terms = [jax.ops.segment_sum(flattened, code_block[which_book].reshape(-1), num_segments=KCODE) for which_book in range(BOOKS)]
        grad_total = grad_total + jnp.stack(book_terms)
        scale_part = lax.optimization_barrier(jnp.sum(decoded * grad_w, axis=0))
        return ((gx_total, grad_total), scale_part)
    start_state = (jnp.zeros((TOKENS, DIN), jnp.float32), jnp.zeros((BOOKS, KCODE, GROUP), jnp.float32))
    (gx_total, grad_total), scale_parts = lax.scan(block_step, start_state, jnp.arange(N_DOUT, dtype=jnp.int32))
    grad_input = gx_total.astype(jnp.bfloat16)
    book_grad = grad_total / loss_scale
    scale_grad = scale_parts.reshape(DOUT) * norm_factor / loss_scale
    new_books, new_book_mean, new_book_var = adam_step(codebooks, book_mean, book_var, book_grad)
    new_scales, new_scale_mean, new_scale_var = adam_step(scales, scale_mean, scale_var, scale_grad)
    return (grad_input, book_grad, new_books, new_book_mean, new_book_var, new_scales, new_scale_mean, new_scale_var)
```

```python
import functools
import math

import jax
import jax.numpy as jnp
from jax import lax
from jax.experimental import pallas as pl
from jax.experimental.pallas import tpu as pltpu
from jax.sharding import PartitionSpec as P

DIN = 8192
DOUT = 28672
KCODE = 256
BOOKS = 2
GROUP = 8
TOKENS = 2048

LANES = 128
LOW = 8
HIGH = KCODE // LOW
VMEM = 56 * 1024 * 1024

beta_one = 0.9
beta_two = 0.999
adam_rate = 0.01
adam_eps = 1e-08
corr_one = 1.0 - 0.9**10
corr_two = 1.0 - 0.999**10


def adam_step(param, mean_old, var_old, gradient):
    mean_new = beta_one * mean_old + (1.0 - beta_one) * gradient
    var_new = beta_two * var_old + (1.0 - beta_two) * gradient * gradient
    update = mean_new / corr_one / (jnp.sqrt(var_new / corr_two) + adam_eps)
    return (param - adam_rate * update, mean_new, var_new)


def split_columns(outs):
    unit = 2 * LANES if outs % (2 * LANES) == 0 else LANES
    units = outs // unit
    last = max(1, units // 7)
    rest = units - last
    pieces = min(3, rest)
    widths = [rest // pieces + (1 if i < rest % pieces else 0) for i in range(pieces)]
    return [w * unit for w in widths if w] + [last * unit]


def largest_tile(size, limit):
    for tile in range(min(size, limit), 0, -1):
        if size % tile == 0 and tile % 8 == 0:
            return tile
    return size


def decode_kernel(tile_groups, width, first, codes_ref, table_ref, coef_ref, weight_ref):
    @pl.loop(0, tile_groups // 8)
    def _(i):
        start = pl.multiple_of(i * 8, 8)
        for q in range(width // LANES):
            cols = pl.ds(q * LANES, LANES)
            code = [codes_ref[b, pl.ds(start, 8), cols] for b in range(BOOKS)]
            coef = jnp.broadcast_to(coef_ref[:, cols], (8, LANES))
            rows = []
            for g in range(8):
                total = None
                for b in range(BOOKS):
                    c = jnp.broadcast_to(code[b][g : g + 1], (8, LANES))
                    low = c & (LANES - 1)
                    value = None
                    for part in range(KCODE // LANES):
                        got = jnp.take_along_axis(
                            table_ref[b, part], low, axis=1, mode="promise_in_bounds"
                        )
                        value = got if part == 0 else jnp.where(c < part * LANES, value, got)
                    total = value if total is None else total + value
                rows.append(total * coef)
            weight_ref[pl.ds(pl.multiple_of(i * 64, 64), 64), cols] = jnp.concatenate(
                rows, axis=0
            ).astype(jnp.bfloat16)


def decode(codes, table, coef, first, width):
    groups = codes.shape[1]
    tile_groups = largest_tile(groups, 64)
    unit = math.gcd(math.gcd(first, width), 512)
    return pl.pallas_call(
        functools.partial(decode_kernel, tile_groups, unit, first),
        grid=(width // unit, groups // tile_groups),
        in_specs=[
            pl.BlockSpec((BOOKS, tile_groups, unit), lambda o, f: (0, f, first // unit + o)),
            pl.BlockSpec(table.shape, lambda o, f: (0, 0, 0, 0)),
            pl.BlockSpec((1, unit), lambda o, f: (0, first // unit + o)),
        ],
        out_specs=pl.BlockSpec((tile_groups * GROUP, unit), lambda o, f: (f, o)),
        out_shape=jax.ShapeDtypeStruct((groups * GROUP, width), jnp.bfloat16),
        compiler_params=pltpu.CompilerParams(vmem_limit_bytes=VMEM),
        cost_estimate=pl.CostEstimate(
            flops=groups * GROUP * width * 6400, bytes_accessed=groups * width * 24, transcendentals=0
        ),
        name="decode_weights",
    )(codes, table, coef)


def piece_places(n, rows):
    places = []
    for d in range(1, (n - 1) // 2 + 1):
        places += [(-d, 0, rows), (d, 0, rows)]
    if n % 2 == 0:
        places += [(-(n // 2), 0, rows // 2), (n // 2, rows // 2, rows - rows // 2)]
    return places


def ring_pieces(own, n):
    forward = [(a, (a + 1) % n) for a in range(n)]
    backward = [((a + 1) % n, a) for a in range(n)]
    rows = own.shape[0]
    left = right = own
    pieces = []
    for _ in range(1, (n - 1) // 2 + 1):
        left = lax.ppermute(left, "din", forward)
        right = lax.ppermute(right, "din", backward)
        pieces += [left, right]
    if n % 2 == 0:
        pieces += [
            lax.ppermute(left[: rows // 2], "din", forward),
            lax.ppermute(right[rows // 2 :], "din", backward),
        ]
    return pieces


def place_pieces(me, n, rows, pieces, out_ref):
    for piece, (shift, skip, count) in zip(pieces, [(0, 0, rows)] + piece_places(n, rows)):
        chunk = lax.rem(me + shift + 2 * n, n)
        out_ref[pl.ds(pl.multiple_of(chunk * rows + skip, 16), count), :] = piece[...]


def histogram_terms(codes, scaled, width):
    spread = jnp.broadcast_to(codes[:, None, :], (8, GROUP, width)).reshape(8 * GROUP, width)
    low = (spread & (LOW - 1)).astype(jnp.bfloat16)
    zero = jnp.bfloat16(0)
    left = jnp.concatenate([jnp.where(low == jnp.bfloat16(v), scaled, zero) for v in range(LOW)], axis=0)
    iota = lax.broadcasted_iota(jnp.int32, (HIGH, width), 0).astype(jnp.bfloat16)
    hits = []
    for g in range(8):
        high = jnp.broadcast_to(codes[g : g + 1] >> 3, (16, width)).astype(jnp.bfloat16)
        for m in range(HIGH // 16):
            hits.append(jnp.where(high == iota[m * 16 : (m + 1) * 16], jnp.bfloat16(1), zero))
    return left, jnp.concatenate(hits, axis=0)


def gradient_kernel(n, tile, width, blocks, count, me_ref, codes_ref, x_ref, weight_ref, coef_ref, *refs):
    pieces, (cot_ref, book_ref, scale_ref, total_ref) = refs[:count], refs[count:]
    step = pl.program_id(0)

    @pl.when(step == 0)
    def _():
        total_ref[...] = jnp.zeros_like(total_ref)
        scale_ref[...] = jnp.zeros_like(scale_ref)
        place_pieces(me_ref[0], n, pieces[0].shape[0], pieces, cot_ref)

    x = jnp.concatenate([x_ref[e] for e in range(blocks)], axis=1) if blocks > 1 else x_ref[0]
    grads = jnp.dot(x, cot_ref[...], preferred_element_type=jnp.float32)
    scale = jnp.zeros((GROUP, width), jnp.float32)
    left, right = [[] for _ in range(BOOKS)], [[] for _ in range(BOOKS)]
    for i in range(tile // 64):
        grad = grads[i * 64 : (i + 1) * 64]
        scaled = (grad * coef_ref[...]).astype(jnp.bfloat16)
        product = grad * weight_ref[i * 64 : (i + 1) * 64, :].astype(jnp.float32)
        scale = scale + jnp.sum(product.reshape(8, GROUP, width), axis=0)
        for b in range(BOOKS):
            masked, hits = histogram_terms(codes_ref[b, i * 8 : (i + 1) * 8, :], scaled, width)
            left[b].append(masked)
            right[b].append(hits)
    scale_ref[...] += scale
    for b in range(BOOKS):
        total_ref[b] += lax.dot_general(
            jnp.concatenate(left[b], axis=1),
            jnp.concatenate(right[b], axis=1),
            (((1,), (1,)), ((), ())),
            preferred_element_type=jnp.float32,
        )

    @pl.when(step == pl.num_programs(0) - 1)
    def _():
        shape = (GROUP, 8 * HIGH)
        column = lax.broadcasted_iota(jnp.int32, shape, 1) // HIGH
        for b in range(BOOKS):
            for v in range(LOW):
                part = jnp.zeros(shape, jnp.float32)
                for g in range(8):
                    block = total_ref[b, pl.ds((v * 8 + g) * GROUP, GROUP), :]
                    part = part + jnp.where(column == g, block, 0.0)
                book_ref[b, pl.ds(v * GROUP, GROUP), :] = part


def gradients(me, n, codes, x, pieces, weights, coef, first, width):
    groups = codes.shape[1]
    blocks, features, tokens_block = x.shape
    tile_groups = largest_tile(groups, 32)
    tile = tile_groups * GROUP
    tokens = blocks * tokens_block
    place = first // width
    if first % width:
        codes = lax.slice_in_dim(codes, first, first + width, axis=2)
        coef = lax.slice_in_dim(coef, first, first + width, axis=1)
        place = 0
    once = pl.Buffered(1)
    return pl.pallas_call(
        functools.partial(gradient_kernel, n, tile, width, blocks, len(pieces)),
        grid=(groups // tile_groups,),
        in_specs=[
            pl.BlockSpec(memory_space=pltpu.SMEM),
            pl.BlockSpec((BOOKS, tile_groups, width), lambda f: (0, f, place)),
            pl.BlockSpec((blocks, tile, tokens_block), lambda f: (0, f, 0)),
            pl.BlockSpec((tile, width), lambda f: (f, 0)),
            pl.BlockSpec((1, width), lambda f: (0, place)),
        ]
        + [pl.BlockSpec(p.shape, lambda f: (0, 0), pipeline_mode=once) for p in pieces],
        out_specs=[
            pl.BlockSpec((tokens, width), lambda f: (0, 0), pipeline_mode=once),
            pl.BlockSpec((BOOKS, LOW * GROUP, 8 * HIGH), lambda f: (0, 0, 0)),
            pl.BlockSpec((GROUP, width), lambda f: (0, 0)),
        ],
        out_shape=[
            jax.ShapeDtypeStruct((tokens, width), jnp.bfloat16),
            jax.ShapeDtypeStruct((BOOKS, LOW * GROUP, 8 * HIGH), jnp.float32),
            jax.ShapeDtypeStruct((GROUP, width), jnp.float32),
        ],
        scratch_shapes=[pltpu.VMEM((BOOKS, LOW * 8 * GROUP, 8 * HIGH), jnp.float32)],
        compiler_params=pltpu.CompilerParams(vmem_limit_bytes=VMEM),
        cost_estimate=pl.CostEstimate(
            flops=3 * 2 * tokens * features * width,
            bytes_accessed=2 * (tokens + 2 * features) * width,
            transcendentals=0,
        ),
        name="weight_gradients",
    )(me, codes, x, weights, coef, *pieces)


def input_gradient_kernel(count, refs):
    left = jnp.concatenate([refs[s][...] for s in range(count)], axis=1)
    right = jnp.concatenate([refs[count + s][...] for s in range(count)], axis=1)
    return lax.dot_general(left, right, (((1,), (1,)), ((), ())), preferred_element_type=jnp.float32)


def early_kernel(count, *refs):
    refs[-1][...] = input_gradient_kernel(count, refs)


def early_input_gradient(cots, weights):
    tokens, features = cots[0].shape[0], weights[0].shape[0]
    tile_t, tile_f = largest_tile(tokens, 512), largest_tile(features, 1024)
    width = sum(c.shape[1] for c in cots)
    return pl.pallas_call(
        functools.partial(early_kernel, len(cots)),
        grid=(features // tile_f, tokens // tile_t),
        in_specs=[pl.BlockSpec((tile_t, c.shape[1]), lambda f, t: (t, 0)) for c in cots]
        + [pl.BlockSpec((tile_f, w.shape[1]), lambda f, t: (f, 0)) for w in weights],
        out_specs=pl.BlockSpec((tile_t, tile_f), lambda f, t: (t, f)),
        out_shape=jax.ShapeDtypeStruct((tokens, features), jnp.float32),
        compiler_params=pltpu.CompilerParams(vmem_limit_bytes=VMEM),
        cost_estimate=pl.CostEstimate(
            flops=2 * tokens * features * width,
            bytes_accessed=4 * tokens * features + 2 * (tokens + features) * width,
            transcendentals=0,
        ),
        name="early_input_gradient",
    )(*cots, *weights)


def last_kernel(n, rows, block, count, me_ref, early_ref, weight_ref, *refs):
    pieces, (out_ref, cot_ref) = refs[:count], refs[count:]

    @pl.when(pl.program_id(0) == 0)
    def _():
        place_pieces(me_ref[0], n, rows, pieces, cot_ref)

    start = pl.multiple_of((2 * pl.program_id(0) + me_ref[1]) * block, 16)
    part = lax.dot_general(
        cot_ref[pl.ds(start, block), :], weight_ref[...], (((1,), (1,)), ((), ())), preferred_element_type=jnp.float32
    )
    out_ref[...] = (early_ref[...] + part).astype(out_ref.dtype)


def last_input_gradient(me, n, block, pieces, weights, early, dtype):
    rows, width = pieces[0].shape
    tokens, features = early.shape
    once = pl.Buffered(1)
    half = tokens // (2 * block)
    return pl.pallas_call(
        functools.partial(last_kernel, n, rows, block, len(pieces)),
        grid_spec=pltpu.PrefetchScalarGridSpec(
            num_scalar_prefetch=1,
            grid=(half,),
            in_specs=[
                pl.BlockSpec((block, features), lambda t, who: (2 * t + who[1], 0)),
                pl.BlockSpec((features, width), lambda t, who: (0, 0), pipeline_mode=once),
            ]
            + [pl.BlockSpec(p.shape, lambda t, who: (0, 0), pipeline_mode=once) for p in pieces],
            out_specs=pl.BlockSpec((block, features), lambda t, who: (t, 0)),
            scratch_shapes=[pltpu.VMEM((tokens, width), jnp.bfloat16)],
        ),
        out_shape=jax.ShapeDtypeStruct((tokens // 2, features), dtype),
        compiler_params=pltpu.CompilerParams(vmem_limit_bytes=VMEM),
        cost_estimate=pl.CostEstimate(
            flops=tokens * features * width, bytes_accessed=3 * tokens * features, transcendentals=0
        ),
        name="last_input_gradient",
    )(me, early, weights, *pieces)


def halving_scatter(keep, got, size):
    me = lax.axis_index("dout")
    bits = size.bit_length() - 1
    tokens, features = keep.shape
    total = keep + got.astype(jnp.float32)
    if bits == 1:
        return total.astype(jnp.bfloat16)
    parts = total.reshape((2,) * (bits - 1) + (2 * tokens // size, features))

    def exchange(part, axis, bit):
        mine = (me >> bit) & 1
        held = lax.dynamic_index_in_dim(part, mine, axis, keepdims=False)
        give = lax.dynamic_index_in_dim(part, 1 - mine, axis, keepdims=False).astype(jnp.bfloat16)
        came = lax.ppermute(give, "dout", [(a, a ^ (1 << bit)) for a in range(size)])
        return held + came.astype(jnp.float32)

    half = features // 2
    one, two = parts[..., :half], parts[..., half:]
    order = list(range(1, bits))
    for step in range(bits - 1):
        up, down = order[step], order[bits - 2 - step]
        left_one = [b for b in reversed(order) if b not in order[:step]]
        left_two = [b for b in reversed(order) if b not in order[bits - 1 - step :]]
        one = exchange(one, left_one.index(up), up)
        two = exchange(two, left_two.index(down), down)
    return jnp.concatenate([one, two], axis=-1).astype(jnp.bfloat16)


def butterfly_sum(value, axis, size):
    if size & (size - 1):
        return lax.psum(value, axis)
    bit = 1
    while bit < size:
        value = value + lax.ppermute(value, axis, [(a, a ^ bit) for a in range(size)])
        bit *= 2
    return value


def local(n_din, n_dout, inputs, cotangent, codes, codebooks, scales, book_mean, book_var, scale_mean, scale_var):
    norm_factor = 1.0 / (2.0 * DOUT) ** 0.5
    loss_scale = (TOKENS * DIN / 4096.0) ** 0.5
    coef = scales * norm_factor
    outs = codes.shape[2]
    me = lax.axis_index("din").astype(jnp.int32).reshape(1)

    if inputs.shape[0] % LANES == 0:
        x = lax.all_gather(inputs.T, "dout", axis=0)
    else:
        x = lax.all_gather(inputs, "dout", axis=0, tiled=True).T[None]

    table = codebooks.astype(jnp.bfloat16).astype(jnp.float32).transpose(0, 2, 1)
    table = table.reshape(BOOKS, GROUP, KCODE // LANES, LANES).transpose(0, 2, 1, 3)
    coef_row = coef.reshape(1, outs)

    widths = split_columns(outs)
    firsts = [sum(widths[:i]) for i in range(len(widths))]
    weights, gathered = [], []
    for s, (first, width) in enumerate(zip(firsts, widths)):
        own = lax.slice_in_dim(cotangent, first, first + width, axis=1)
        if s >= 2 and n_din > 1:
            own, _ = lax.optimization_barrier((own, gathered[s - 2][1]))
        gathered.append([own] + ring_pieces(own, n_din))
        weights.append(decode(codes, table, coef_row, first, width))

    books, scale_parts, cots = [], [], []

    def run_gradients(s, after):
        row = coef_row if after is None else lax.optimization_barrier((coef_row, after))[0]
        cot, book, scale = gradients(me, n_din, codes, x, gathered[s], weights[s], row, firsts[s], widths[s])
        books.append(book)
        scale_parts.append(scale)
        cots.append(cot)

    final = len(widths) - 1
    for s in range(final):
        run_gradients(s, scale_parts[-1] if scale_parts else None)
    early = early_input_gradient(cots, weights[:final])
    block = inputs.shape[0]
    if n_dout > 1 and n_dout & (n_dout - 1) == 0:
        core = lax.axis_index("dout").astype(jnp.int32) & 1
        both_me = [jnp.stack([me[0], 1 - core]), jnp.stack([me[0], core])]
        give = last_input_gradient(both_me[0], n_din, block, gathered[final], weights[final], early, jnp.bfloat16)
        got = lax.ppermute(give, "dout", [(a, a ^ 1) for a in range(n_dout)])
        keep = last_input_gradient(both_me[1], n_din, block, gathered[final], weights[final], early, jnp.float32)
        run_gradients(final, keep[:1, :LANES])
        grad_input = halving_scatter(keep, got, n_dout)
    else:
        run_gradients(final, early[:1, :LANES])
        rows = early_input_gradient(cots, weights)
        grad_input = lax.psum_scatter(rows, "dout", scatter_dimension=0, tiled=True).astype(jnp.bfloat16)

    book = sum(books[1:], books[0]).reshape(BOOKS, LOW, GROUP, 8, HIGH).sum(axis=3)
    book = book.transpose(0, 3, 1, 2).reshape(BOOKS * KCODE * GROUP)
    scale_total = jnp.concatenate([jnp.sum(part, axis=0) for part in scale_parts]) / coef
    both = butterfly_sum(jnp.concatenate([book, scale_total]), "din", n_din)
    grad_sums = butterfly_sum(both[: book.shape[0]], "dout", n_dout).reshape(BOOKS, KCODE, GROUP)
    scale_sums = both[book.shape[0] :]

    book_grad = grad_sums / loss_scale
    scale_grad = scale_sums * norm_factor / loss_scale
    new_books, new_book_mean, new_book_var = adam_step(codebooks, book_mean, book_var, book_grad)
    new_scales, new_scale_mean, new_scale_var = adam_step(scales, scale_mean, scale_var, scale_grad)
    return (
        grad_input,
        book_grad,
        new_books,
        new_book_mean,
        new_book_var,
        new_scales,
        new_scale_mean,
        new_scale_var,
    )


def solution(mesh):
    in_specs = (
        P("dout", "din"),
        P("din", "dout"),
        P(None, "din", "dout"),
        P(),
        P("dout"),
        P(),
        P(),
        P("dout"),
        P("dout"),
    )
    out_specs = (P("dout", "din"), P(), P(), P(), P(), P("dout"), P("dout"), P("dout"))
    body = functools.partial(local, mesh.shape["din"], mesh.shape["dout"])
    return jax.shard_map(body, mesh=mesh, in_specs=in_specs, out_specs=out_specs, check_vma=False)
```

```python
import functools
import math

import jax
import jax.numpy as jnp
from jax import lax
from jax.experimental import pallas as pl
from jax.experimental.pallas import tpu as pltpu
from jax.sharding import PartitionSpec as P

DIN = 8192
DOUT = 28672
KCODE = 256
BOOKS = 2
GROUP = 8
TOKENS = 2048

LANES = 128
LOW = 8
HIGH = KCODE // LOW
VMEM = 56 * 1024 * 1024

beta_one = 0.9
beta_two = 0.999
adam_rate = 0.01
adam_eps = 1e-08
corr_one = 1.0 - 0.9**10
corr_two = 1.0 - 0.999**10


def adam_step(param, mean_old, var_old, gradient):
    mean_new = beta_one * mean_old + (1.0 - beta_one) * gradient
    var_new = beta_two * var_old + (1.0 - beta_two) * gradient * gradient
    update = mean_new / corr_one / (jnp.sqrt(var_new / corr_two) + adam_eps)
    return (param - adam_rate * update, mean_new, var_new)


def split_columns(outs):
    unit = next((u for u in (4 * LANES, 2 * LANES) if outs % u == 0), LANES)
    units = outs // unit
    shares = (2, 2, 2, 1)
    ends = [round(units * sum(shares[: i + 1]) / sum(shares)) for i in range(len(shares))]
    widths = [(end - start) * unit for start, end in zip([0] + ends, ends)]
    return [width for width in widths if width]


def largest_tile(size, limit):
    for tile in range(min(size, limit), 0, -1):
        if size % tile == 0 and tile % 8 == 0:
            return tile
    return size


def packed_table(codebooks):
    rounded = codebooks.astype(jnp.bfloat16).astype(jnp.float32).transpose(0, 2, 1)
    unit = jnp.maximum(jnp.max(jnp.abs(rounded)), 1e-30) / 32767.0
    fixed = jnp.round(rounded / unit).astype(jnp.int32)
    return fixed[..., :LANES] * 65536 + (fixed[..., LANES:] & 65535), unit


def decode_kernel(tile_groups, width, codes_ref, table_ref, coef_ref, _, weight_ref):
    @pl.loop(0, tile_groups // 8)
    def _(i):
        start = pl.multiple_of(i * 8, 8)
        for q in range(width // LANES):
            cols = pl.ds(q * LANES, LANES)
            code = [codes_ref[b, pl.ds(start, 8), cols] for b in range(BOOKS)]
            coef = jnp.broadcast_to(coef_ref[:, cols], (8, LANES))
            rows = []
            for g in range(8):
                total = None
                for b in range(BOOKS):
                    c = jnp.broadcast_to(code[b][g : g + 1], (8, LANES))
                    word = jnp.take_along_axis(table_ref[b], c & (LANES - 1), axis=1, mode="promise_in_bounds")
                    value = (word << ((c & LANES) >> 3)) >> 16
                    total = value if total is None else total + value
                rows.append(total.astype(jnp.float32) * coef)
            weight_ref[pl.ds(pl.multiple_of(i * 64, 64), 64), cols] = jnp.concatenate(
                rows, axis=0
            ).astype(jnp.bfloat16)


def decode(codes, table, coef, after, first, width):
    groups = codes.shape[1]
    tile_groups = largest_tile(groups, 64)
    unit = math.gcd(math.gcd(first, width), 512)
    return pl.pallas_call(
        functools.partial(decode_kernel, tile_groups, unit),
        grid=(width // unit, groups // tile_groups),
        in_specs=[
            pl.BlockSpec((BOOKS, tile_groups, unit), lambda o, f: (0, f, first // unit + o)),
            pl.BlockSpec(table.shape, lambda o, f: (0, 0, 0)),
            pl.BlockSpec((1, unit), lambda o, f: (0, first // unit + o)),
            pl.BlockSpec(memory_space=pl.ANY),
        ],
        out_specs=pl.BlockSpec((tile_groups * GROUP, unit), lambda o, f: (f, o)),
        out_shape=jax.ShapeDtypeStruct((groups * GROUP, width), jnp.bfloat16),
        compiler_params=pltpu.CompilerParams(vmem_limit_bytes=VMEM),
        cost_estimate=pl.CostEstimate(
            flops=groups * GROUP * width * 9000, bytes_accessed=groups * width * 24, transcendentals=0
        ),
        name="decode_weights",
    )(codes, table, coef, after)


def piece_places(n, rows):
    places = []
    for d in range(1, (n - 1) // 2 + 1):
        places += [(-d, 0, rows), (d, 0, rows)]
    if n % 2 == 0:
        places += [(-(n // 2), 0, rows // 2), (n // 2, rows // 2, rows - rows // 2)]
    return places


class Ring:
    def __init__(self, n, rows):
        self.n, self.rows = n, rows
        self.forward = [(a, (a + 1) % n) for a in range(n)]
        self.backward = [((a + 1) % n, a) for a in range(n)]

    def begin(self, own):
        self.pieces = [own]
        self.left = self.right = own
        for _ in range(1, (self.n - 1) // 2 + 1):
            self.left = lax.ppermute(self.left, "din", self.forward)
            self.right = lax.ppermute(self.right, "din", self.backward)
            self.pieces += [self.left, self.right]

    def hold(self, gate):
        first = len(self.pieces) > 1
        held, gate = lax.optimization_barrier((self.pieces, gate))
        self.pieces = list(held)
        if first:
            self.left, self.right = self.pieces[-2:]
        return gate

    def finish(self, following):
        if self.n % 2 == 0:
            half = self.rows // 2
            halves, following = lax.optimization_barrier(((self.left[:half], self.right[half:]), following))
            self.pieces += [
                lax.ppermute(halves[0], "din", self.forward),
                lax.ppermute(halves[1], "din", self.backward),
            ]
        return following


def transpose_kernel(in_ref, out_ref):
    out_ref[...] = in_ref[...].T


def transpose(block):
    rows, columns = block.shape
    tile = largest_tile(columns, 512)
    return pl.pallas_call(
        transpose_kernel,
        grid=(columns // tile,),
        in_specs=[pl.BlockSpec((rows, tile), lambda c: (0, c))],
        out_specs=pl.BlockSpec((tile, rows), lambda c: (c, 0)),
        out_shape=jax.ShapeDtypeStruct((columns, rows), block.dtype),
        name="transpose_inputs",
    )(block)


def place_pieces(me, n, rows, pieces, out_ref):
    for piece, (shift, skip, count) in zip(pieces, [(0, 0, rows)] + piece_places(n, rows)):
        chunk = lax.rem(me + shift + 2 * n, n)
        out_ref[pl.ds(pl.multiple_of(chunk * rows + skip, 16), count), :] = piece[...]


def histogram_terms(codes, scaled, width):
    spread = jnp.broadcast_to(codes[:, None, :], (8, GROUP, width)).reshape(8 * GROUP, width)
    low = (spread & (LOW - 1)).astype(jnp.bfloat16)
    zero = jnp.bfloat16(0)
    left = jnp.concatenate([jnp.where(low == jnp.bfloat16(v), scaled, zero) for v in range(LOW)], axis=0)
    iota = lax.broadcasted_iota(jnp.int32, (HIGH, width), 0).astype(jnp.bfloat16)
    hits = []
    for g in range(8):
        high = jnp.broadcast_to(codes[g : g + 1] >> 3, (16, width)).astype(jnp.bfloat16)
        for m in range(HIGH // 16):
            hits.append(jnp.where(high == iota[m * 16 : (m + 1) * 16], jnp.bfloat16(1), zero))
    return left, jnp.concatenate(hits, axis=0)


def gradient_kernel(n, tile, width, blocks, count, parts, me_ref, x_ref, weight_ref, _, *refs):
    code_refs, coef_refs, refs = refs[:parts], refs[parts : 2 * parts], refs[2 * parts :]
    pieces, (cot_ref, book_ref, scale_ref, total_ref) = refs[:count], refs[count:]
    step = pl.program_id(0)

    @pl.when(step == 0)
    def _():
        total_ref[...] = jnp.zeros_like(total_ref)
        scale_ref[...] = jnp.zeros_like(scale_ref)
        place_pieces(me_ref[0], n, pieces[0].shape[0], pieces, cot_ref)

    x = jnp.concatenate([x_ref[e] for e in range(blocks)], axis=1) if blocks > 1 else x_ref[0]
    grads = jnp.dot(x, cot_ref[...], preferred_element_type=jnp.float32)
    coef = jnp.concatenate([ref[...] for ref in coef_refs], axis=1)
    scale = jnp.zeros((GROUP, width), jnp.float32)
    left, right = [[] for _ in range(BOOKS)], [[] for _ in range(BOOKS)]
    for i in range(tile // 64):
        grad = grads[i * 64 : (i + 1) * 64]
        scaled = (grad * coef).astype(jnp.bfloat16)
        product = grad * weight_ref[i * 64 : (i + 1) * 64, :].astype(jnp.float32)
        scale = scale + jnp.sum(product.reshape(8, GROUP, width), axis=0)
        for b in range(BOOKS):
            codes = jnp.concatenate([ref[b, i * 8 : (i + 1) * 8, :] for ref in code_refs], axis=1)
            masked, hits = histogram_terms(codes, scaled, width)
            left[b].append(masked)
            right[b].append(hits)
    scale_ref[...] += scale
    for b in range(BOOKS):
        total_ref[b] += lax.dot_general(
            jnp.concatenate(left[b], axis=1),
            jnp.concatenate(right[b], axis=1),
            (((1,), (1,)), ((), ())),
            preferred_element_type=jnp.float32,
        )

    @pl.when(step == pl.num_programs(0) - 1)
    def _():
        shape = (GROUP, 8 * HIGH)
        column = lax.broadcasted_iota(jnp.int32, shape, 1) // HIGH
        for b in range(BOOKS):
            for v in range(LOW):
                part = jnp.zeros(shape, jnp.float32)
                for g in range(8):
                    block = total_ref[b, pl.ds((v * 8 + g) * GROUP, GROUP), :]
                    part = part + jnp.where(column == g, block, 0.0)
                book_ref[b, pl.ds(v * GROUP, GROUP), :] = part


def gradients(me, n, codes, x, pieces, weights, coef, after, first, width):
    groups = codes.shape[1]
    blocks, features, tokens_block = x.shape
    tile_groups = largest_tile(groups, 32)
    tile = tile_groups * GROUP
    tokens = blocks * tokens_block
    unit = math.gcd(first, width)
    parts = width // unit
    places = [first // unit + p for p in range(parts)]
    once = pl.Buffered(1)
    return pl.pallas_call(
        functools.partial(gradient_kernel, n, tile, width, blocks, len(pieces), parts),
        grid=(groups // tile_groups,),
        in_specs=[
            pl.BlockSpec(memory_space=pltpu.SMEM),
            pl.BlockSpec((blocks, tile, tokens_block), lambda f: (0, f, 0)),
            pl.BlockSpec((tile, width), lambda f: (f, 0)),
            pl.BlockSpec(memory_space=pl.ANY),
        ]
        + [pl.BlockSpec((BOOKS, tile_groups, unit), lambda f, p=p: (0, f, p)) for p in places]
        + [pl.BlockSpec((1, unit), lambda f, p=p: (0, p)) for p in places]
        + [pl.BlockSpec(p.shape, lambda f: (0, 0), pipeline_mode=once) for p in pieces],
        out_specs=[
            pl.BlockSpec((tokens, width), lambda f: (0, 0), pipeline_mode=once),
            pl.BlockSpec((BOOKS, LOW * GROUP, 8 * HIGH), lambda f: (0, 0, 0)),
            pl.BlockSpec((GROUP, width), lambda f: (0, 0)),
        ],
        out_shape=[
            jax.ShapeDtypeStruct((tokens, width), jnp.bfloat16),
            jax.ShapeDtypeStruct((BOOKS, LOW * GROUP, 8 * HIGH), jnp.float32),
            jax.ShapeDtypeStruct((GROUP, width), jnp.float32),
        ],
        scratch_shapes=[pltpu.VMEM((BOOKS, LOW * 8 * GROUP, 8 * HIGH), jnp.float32)],
        compiler_params=pltpu.CompilerParams(vmem_limit_bytes=VMEM),
        cost_estimate=pl.CostEstimate(
            flops=9 * tokens * features * width,
            bytes_accessed=2 * (tokens + 2 * features) * width,
            transcendentals=0,
        ),
        name="weight_gradients",
    )(me, x, weights, after, *([codes] * parts), *([coef] * parts), *pieces)


def input_gradient_kernel(count, refs):
    left = jnp.concatenate([refs[s][...] for s in range(count)], axis=1)
    right = jnp.concatenate([refs[count + s][...] for s in range(count)], axis=1)
    return lax.dot_general(left, right, (((1,), (1,)), ((), ())), preferred_element_type=jnp.float32)


def early_kernel(count, added, *refs):
    total = input_gradient_kernel(count, refs)
    refs[-1][...] = refs[2 * count][...] + total if added else total


def early_input_gradient(cots, weights, total, after):
    tokens, features = cots[0].shape[0], weights[0].shape[0]
    tile_t, tile_f = largest_tile(tokens, 512), largest_tile(features, 1024)
    width = sum(c.shape[1] for c in cots)
    out_spec = pl.BlockSpec((tile_t, tile_f), lambda f, t: (t, f))
    args = [*cots, *weights] + ([] if total is None else [total]) + [after]
    return pl.pallas_call(
        functools.partial(early_kernel, len(cots), total is not None),
        grid=(features // tile_f, tokens // tile_t),
        in_specs=[pl.BlockSpec((tile_t, c.shape[1]), lambda f, t: (t, 0)) for c in cots]
        + [pl.BlockSpec((tile_f, w.shape[1]), lambda f, t: (f, 0)) for w in weights]
        + ([] if total is None else [out_spec])
        + [pl.BlockSpec(memory_space=pl.ANY)],
        out_specs=out_spec,
        out_shape=jax.ShapeDtypeStruct((tokens, features), jnp.float32),
        input_output_aliases={} if total is None else {2 * len(cots): 0},
        compiler_params=pltpu.CompilerParams(vmem_limit_bytes=VMEM),
        cost_estimate=pl.CostEstimate(
            flops=3 * tokens * features * width,
            bytes_accessed=4 * tokens * features + 2 * (tokens + features) * width,
            transcendentals=0,
        ),
        name="early_input_gradient",
    )(*args)


def last_kernel(n, rows, block, fulls, count, me_ref, early_ref, *refs):
    cots, weights, refs = refs[:fulls], refs[fulls : 2 * fulls + 1], refs[2 * fulls + 1 :]
    pieces, (one_ref, two_ref, cot_ref) = refs[:count], refs[count:]

    @pl.when(pl.program_id(0) == 0)
    def _():
        place_pieces(me_ref[0], n, rows, pieces, cot_ref)

    start = pl.multiple_of((2 * pl.program_id(0) + me_ref[1]) * block, 16)
    left = jnp.concatenate([ref[...] for ref in cots] + [cot_ref[pl.ds(start, block), :]], axis=1)
    half = one_ref.shape[1]
    for out_ref, columns in ((one_ref, slice(0, half)), (two_ref, slice(half, 2 * half))):
        right = jnp.concatenate([ref[columns, :] for ref in weights], axis=1)
        part = lax.dot_general(left, right, (((1,), (1,)), ((), ())), preferred_element_type=jnp.float32)
        out_ref[...] = (early_ref[:, columns] + part).astype(out_ref.dtype)


def last_input_gradient(me, n, block, cots, pieces, weights, early, dtype):
    rows = pieces[0].shape[0]
    tokens, features = early.shape
    once = pl.Buffered(1)
    half = tokens // (2 * block)
    width = sum(w.shape[1] for w in weights)
    return pl.pallas_call(
        functools.partial(last_kernel, n, rows, block, len(cots), len(pieces)),
        grid_spec=pltpu.PrefetchScalarGridSpec(
            num_scalar_prefetch=1,
            grid=(half,),
            in_specs=[pl.BlockSpec((block, features), lambda t, who: (2 * t + who[1], 0))]
            + [pl.BlockSpec((block, c.shape[1]), lambda t, who: (2 * t + who[1], 0)) for c in cots]
            + [pl.BlockSpec(w.shape, lambda t, who: (0, 0), pipeline_mode=once) for w in weights]
            + [pl.BlockSpec(p.shape, lambda t, who: (0, 0), pipeline_mode=once) for p in pieces],
            out_specs=[pl.BlockSpec((block, features // 2), lambda t, who: (t, 0))] * 2,
            scratch_shapes=[pltpu.VMEM((tokens, pieces[0].shape[1]), jnp.bfloat16)],
        ),
        out_shape=[jax.ShapeDtypeStruct((tokens // 2, features // 2), dtype)] * 2,
        compiler_params=pltpu.CompilerParams(vmem_limit_bytes=VMEM),
        cost_estimate=pl.CostEstimate(
            flops=2 * tokens * features * width, bytes_accessed=3 * tokens * features, transcendentals=0
        ),
        name="last_input_gradient",
    )(me, early, *cots, *weights, *pieces)


class HalvingScatter:
    def __init__(self, terms, size):
        self.size = size
        self.me = lax.axis_index("dout")
        self.order = list(range(1, size.bit_length() - 1))
        self.step = 0
        rows = 2 * terms[0][0].shape[0] // size
        shape = (2,) * len(self.order) + (rows, terms[0][0].shape[1])
        self.terms = [[t.reshape(shape) for t in half] for half in terms]

    @staticmethod
    def total(terms):
        return sum((t.astype(jnp.float32) for t in terms[1:]), terms[0].astype(jnp.float32))

    def exchange(self, gate=None):
        gives, helds = [], []
        for which in range(2):
            axis, bit = self.place(which)
            mine = (self.me >> bit) & 1
            terms = self.terms[which]
            helds.append([lax.dynamic_index_in_dim(t, mine, axis, keepdims=False) for t in terms])
            give = self.total([lax.dynamic_index_in_dim(t, 1 - mine, axis, keepdims=False) for t in terms])
            gives.append(give.astype(jnp.bfloat16))
        if gate is not None:
            gives, gate = lax.optimization_barrier((gives, gate))
        for which in range(2):
            bit = self.place(which)[1]
            came = lax.ppermute(gives[which], "dout", [(a, a ^ (1 << bit)) for a in range(self.size)])
            self.terms[which] = helds[which] + [came]
        self.step += 1
        return gives if gate is None else gate

    def place(self, which):
        order = self.order if which == 0 else self.order[::-1]
        left = [b for b in reversed(self.order) if b not in order[: self.step]]
        return left.index(order[self.step]), order[self.step]

    def finish(self, gate):
        while self.step < len(self.order):
            gate = self.exchange(gate)
        return jnp.concatenate([self.total(t) for t in self.terms], axis=-1).astype(jnp.bfloat16), gate


def butterfly_sum(value, axis, size):
    if size & (size - 1):
        return lax.psum(value, axis)

    def other(bits):
        return lax.ppermute(value, axis, [(a, a ^ bits) for a in range(size)])

    bit = 1
    while bit < size:
        if 2 * bit < size:
            near, far, both = other(bit), other(2 * bit), other(3 * bit)
            value = (value + near) + (far + both)
            bit *= 4
        else:
            value = value + other(bit)
            bit *= 2
    return value


def local(n_din, n_dout, inputs, cotangent, codes, codebooks, scales, book_mean, book_var, scale_mean, scale_var):
    norm_factor = 1.0 / (2.0 * DOUT) ** 0.5
    loss_scale = (TOKENS * DIN / 4096.0) ** 0.5
    coef = scales * norm_factor
    outs = codes.shape[2]
    me = lax.axis_index("din").astype(jnp.int32).reshape(1)

    if inputs.shape[0] % LANES == 0:
        x = lax.all_gather(transpose(inputs), "dout", axis=0, tiled=True).reshape(n_dout, inputs.shape[1], inputs.shape[0])
    else:
        x = lax.all_gather(inputs, "dout", axis=0, tiled=True).T[None]

    table, unit = packed_table(codebooks)
    coef_row = coef.reshape(1, outs)
    unit_row = coef_row * unit

    widths = split_columns(outs)
    firsts = [sum(widths[:i]) for i in range(len(widths))]
    final = len(widths) - 1
    owns = [lax.slice_in_dim(cotangent, f, f + w, axis=1) for f, w in zip(firsts, widths)]
    rings = [Ring(n_din, own.shape[0]) for own in owns]
    weights = [None] * len(widths)
    books, scale_parts, cots = [], [], []

    def run_decode(s, after):
        weights[s] = decode(codes, table, unit_row, after, firsts[s], widths[s])

    def run_gradients(s, after):
        cot, book, scale = gradients(
            me, n_din, codes, x, rings[s].pieces, weights[s], coef_row, after, firsts[s], widths[s]
        )
        cots.append(cot)
        books.append(book)
        scale_parts.append(scale)
        return scale

    rings[0].begin(owns[0])
    for s in range(min(2, final + 1)):
        run_decode(s, coef_row)
    early, summed, gate = None, 0, weights[min(1, final)]
    for s in range(final + 1):
        gate = rings[s].hold(gate)
        if s == 0:
            weights[min(1, final)] = gate
        gate = rings[s].finish(gate)
        if s == 0 and final >= 2:
            run_decode(2, gate)
            gate = weights[2]
        if 0 < s < max(2, final):
            early = early_input_gradient(cots[summed:], weights[summed:s], early, gate)
            summed, gate = s, early
        if s < final:
            gate = rings[s].hold(gate)
            owns[s + 1], gate = lax.optimization_barrier((owns[s + 1], gate))
            if s > 0:
                early = gate
            elif final >= 2:
                weights[2] = gate
            rings[s + 1].begin(owns[s + 1])
            gate = run_gradients(s, gate)
            if s == 0:
                for later in range(3, final + 1):
                    run_decode(later, gate)
                    gate = weights[later]

    block = inputs.shape[0]
    if early is not None and n_dout > 1 and n_dout & (n_dout - 1) == 0:
        core = lax.axis_index("dout").astype(jnp.int32) & 1
        both_me = [jnp.stack([me[0], 1 - core]), jnp.stack([me[0], core])]
        pieces = rings[final].pieces
        rest = (n_din, block, cots[summed:], pieces, weights[summed:], early)
        give = last_input_gradient(both_me[0], *rest, jnp.bfloat16)
        got = [lax.ppermute(half, "dout", [(a, a ^ 1) for a in range(n_dout)]) for half in give]
        keep = last_input_gradient(both_me[1], *rest, jnp.float32)
        scatter = HalvingScatter([[k, g] for k, g in zip(keep, got)], n_dout)
        gate = keep[0]
        if n_dout > 2:
            gate = lax.optimization_barrier(scatter.exchange())[0]
        run_gradients(final, gate)
        grad_input, books[-1] = scatter.finish(books[-1])
    else:
        run_gradients(final, gate)
        rows = early_input_gradient(cots, weights, None, gate)
        grad_input = lax.psum_scatter(rows, "dout", scatter_dimension=0, tiled=True).astype(jnp.bfloat16)

    book = sum(books[1:], books[0]).reshape(BOOKS, LOW, GROUP, 8, HIGH).sum(axis=3)
    book = book.transpose(0, 3, 1, 2).reshape(BOOKS * KCODE * GROUP)
    scale_total = jnp.concatenate([jnp.sum(part, axis=0) for part in scale_parts]) / coef
    both = butterfly_sum(jnp.concatenate([book, scale_total]), "din", n_din)
    grad_sums = butterfly_sum(both[: book.shape[0]], "dout", n_dout).reshape(BOOKS, KCODE, GROUP)
    scale_sums = both[book.shape[0] :]

    book_grad = grad_sums / loss_scale
    scale_grad = scale_sums * norm_factor / loss_scale
    new_books, new_book_mean, new_book_var = adam_step(codebooks, book_mean, book_var, book_grad)
    new_scales, new_scale_mean, new_scale_var = adam_step(scales, scale_mean, scale_var, scale_grad)
    return (
        grad_input,
        book_grad,
        new_books,
        new_book_mean,
        new_book_var,
        new_scales,
        new_scale_mean,
        new_scale_var,
    )


def solution(mesh):
    in_specs = (
        P("dout", "din"),
        P("din", "dout"),
        P(None, "din", "dout"),
        P(),
        P("dout"),
        P(),
        P(),
        P("dout"),
        P("dout"),
    )
    out_specs = (P("dout", "din"), P(), P(), P(), P(), P("dout"), P("dout"), P("dout"))
    body = functools.partial(local, mesh.shape["din"], mesh.shape["dout"])
    return jax.shard_map(body, mesh=mesh, in_specs=in_specs, out_specs=out_specs, check_vma=False)
```

```python
import functools
import math

import jax
import jax.numpy as jnp
from jax import lax
from jax.experimental import pallas as pl
from jax.experimental.pallas import tpu as pltpu
from jax.sharding import PartitionSpec as P

DIN = 8192
DOUT = 28672
KCODE = 256
BOOKS = 2
GROUP = 8
TOKENS = 2048

LANES = 128
LOW = 8
HIGH = KCODE // LOW
VMEM = 56 * 1024 * 1024

beta_one = 0.9
beta_two = 0.999
adam_rate = 0.01
adam_eps = 1e-08
corr_one = 1.0 - 0.9**10
corr_two = 1.0 - 0.999**10


def adam_step(param, mean_old, var_old, gradient):
    mean_new = beta_one * mean_old + (1.0 - beta_one) * gradient
    var_new = beta_two * var_old + (1.0 - beta_two) * gradient * gradient
    update = mean_new / corr_one / (jnp.sqrt(var_new / corr_two) + adam_eps)
    return (param - adam_rate * update, mean_new, var_new)


def split_columns(outs):
    unit = next((u for u in (2 * LANES,) if outs % u == 0), LANES)
    units = outs // unit
    shares = (5, 5, 4)
    ends = [round(units * sum(shares[: i + 1]) / sum(shares)) for i in range(len(shares))]
    widths = [(end - start) * unit for start, end in zip([0] + ends, ends)]
    return [width for width in widths if width]


def largest_tile(size, limit):
    for tile in range(min(size, limit), 0, -1):
        if size % tile == 0 and tile % 8 == 0:
            return tile
    return size


def packed_table(codebooks):
    rounded = codebooks.astype(jnp.bfloat16).astype(jnp.float32).transpose(0, 2, 1)
    unit = jnp.maximum(jnp.max(jnp.abs(rounded)), 1e-30) / 32767.0
    fixed = jnp.round(rounded / unit).astype(jnp.int32)
    return fixed[..., :LANES] * 65536 + (fixed[..., LANES:] & 65535), unit


def decode_kernel(tile_groups, width, codes_ref, table_ref, coef_ref, _, weight_ref):
    @pl.loop(0, tile_groups // 8)
    def _(i):
        start = pl.multiple_of(i * 8, 8)
        for q in range(width // LANES):
            cols = pl.ds(q * LANES, LANES)
            code = [codes_ref[b, pl.ds(start, 8), cols] for b in range(BOOKS)]
            coef = jnp.broadcast_to(coef_ref[:, cols], (8, LANES))
            rows = []
            for g in range(8):
                total = None
                for b in range(BOOKS):
                    c = jnp.broadcast_to(code[b][g : g + 1], (8, LANES))
                    word = jnp.take_along_axis(table_ref[b], c & (LANES - 1), axis=1, mode="promise_in_bounds")
                    value = (word << ((c & LANES) >> 3)) >> 16
                    total = value if total is None else total + value
                rows.append(total.astype(jnp.float32) * coef)
            weight_ref[pl.ds(pl.multiple_of(i * 64, 64), 64), cols] = jnp.concatenate(
                rows, axis=0
            ).astype(jnp.bfloat16)


def decode(codes, table, coef, after, first, width):
    groups = codes.shape[1]
    tile_groups = largest_tile(groups, 64)
    unit = math.gcd(first, width)
    if unit > 12 * LANES:
        unit = math.gcd(unit, 4 * LANES)
    return pl.pallas_call(
        functools.partial(decode_kernel, tile_groups, unit),
        grid=(width // unit, groups // tile_groups),
        in_specs=[
            pl.BlockSpec((BOOKS, tile_groups, unit), lambda o, f: (0, f, first // unit + o)),
            pl.BlockSpec(table.shape, lambda o, f: (0, 0, 0)),
            pl.BlockSpec((1, unit), lambda o, f: (0, first // unit + o)),
            pl.BlockSpec(memory_space=pl.ANY),
        ],
        out_specs=pl.BlockSpec((tile_groups * GROUP, unit), lambda o, f: (f, o)),
        out_shape=jax.ShapeDtypeStruct((groups * GROUP, width), jnp.bfloat16),
        compiler_params=pltpu.CompilerParams(vmem_limit_bytes=VMEM),
        cost_estimate=pl.CostEstimate(
            flops=groups * GROUP * width * 9000, bytes_accessed=groups * width * 24, transcendentals=0
        ),
        name="decode_weights",
    )(codes, table, coef, after)


def piece_places(n, rows):
    places = []
    for d in range(1, (n - 1) // 2 + 1):
        places += [(-d, 0, rows), (d, 0, rows)]
    if n % 2 == 0:
        places += [(-(n // 2), 0, rows)]
    return places


class Ring:
    def __init__(self, n, rows):
        self.n, self.rows = n, rows
        self.forward = [(a, (a + 1) % n) for a in range(n)]
        self.backward = [((a + 1) % n, a) for a in range(n)]

    def begin(self, own):
        self.pieces = [own]
        self.left = self.right = own
        for _ in range(1, (self.n - 1) // 2 + 1):
            self.left = lax.ppermute(self.left, "din", self.forward)
            self.right = lax.ppermute(self.right, "din", self.backward)
            self.pieces += [self.left, self.right]

    def hold(self, gate):
        first = len(self.pieces) > 1
        held, gate = lax.optimization_barrier((self.pieces, gate))
        self.pieces = list(held)
        if first:
            self.left = self.pieces[-2]
        return gate

    def finish(self):
        if self.n % 2 == 0:
            self.pieces.append(lax.ppermute(self.left, "din", self.forward))


def transpose_kernel(in_ref, out_ref):
    out_ref[...] = in_ref[...].T


def transpose(block):
    rows, columns = block.shape
    tile = largest_tile(columns, 512)
    return pl.pallas_call(
        transpose_kernel,
        grid=(columns // tile,),
        in_specs=[pl.BlockSpec((rows, tile), lambda c: (0, c))],
        out_specs=pl.BlockSpec((tile, rows), lambda c: (c, 0)),
        out_shape=jax.ShapeDtypeStruct((columns, rows), block.dtype),
        name="transpose_inputs",
    )(block)


def place_pieces(me, n, rows, pieces, out_ref):
    for piece, (shift, skip, count) in zip(pieces, [(0, 0, rows)] + piece_places(n, rows)):
        chunk = lax.rem(me + shift + 2 * n, n)
        out_ref[pl.ds(pl.multiple_of(chunk * rows + skip, 16), count), :] = piece[...]


def histogram_terms(codes, scaled, width):
    spread = jnp.broadcast_to(codes[:, None, :], (8, GROUP, width)).reshape(8 * GROUP, width)
    low = (spread & (LOW - 1)).astype(jnp.bfloat16)
    zero = jnp.bfloat16(0)
    left = jnp.concatenate([jnp.where(low == jnp.bfloat16(v), scaled, zero) for v in range(LOW)], axis=0)
    iota = lax.broadcasted_iota(jnp.int32, (HIGH, width), 0).astype(jnp.bfloat16)
    hits = []
    for g in range(8):
        high = jnp.broadcast_to(codes[g : g + 1] >> 3, (16, width)).astype(jnp.bfloat16)
        for m in range(HIGH // 16):
            hits.append(jnp.where(high == iota[m * 16 : (m + 1) * 16], jnp.bfloat16(1), zero))
    return left, jnp.concatenate(hits, axis=0)


def gradient_kernel(n, tile, width, blocks, count, parts, me_ref, x_ref, weight_ref, _, *refs):
    code_refs, coef_refs, refs = refs[:parts], refs[parts : 2 * parts], refs[2 * parts :]
    pieces, refs = refs[:count], refs[count:]
    cot_ref = refs[0] if count > 1 else pieces[0]
    book_ref, scale_ref, total_ref = refs[-3:]
    step = pl.program_id(0)

    @pl.when(step == 0)
    def _():
        total_ref[...] = jnp.zeros_like(total_ref)
        scale_ref[...] = jnp.zeros_like(scale_ref)
        if count > 1:
            place_pieces(me_ref[0], n, pieces[0].shape[0], pieces, cot_ref)

    x = jnp.concatenate([x_ref[e] for e in range(blocks)], axis=1) if blocks > 1 else x_ref[0]
    grads = jnp.dot(x, cot_ref[...], preferred_element_type=jnp.float32)
    coef = jnp.concatenate([ref[...] for ref in coef_refs], axis=1)
    scale = jnp.zeros((GROUP, width), jnp.float32)
    left, right = [[] for _ in range(BOOKS)], [[] for _ in range(BOOKS)]
    for i in range(tile // 64):
        grad = grads[i * 64 : (i + 1) * 64]
        scaled = (grad * coef).astype(jnp.bfloat16)
        product = grad * weight_ref[i * 64 : (i + 1) * 64, :].astype(jnp.float32)
        scale = scale + jnp.sum(product.reshape(8, GROUP, width), axis=0)
        for b in range(BOOKS):
            codes = jnp.concatenate([ref[b, i * 8 : (i + 1) * 8, :] for ref in code_refs], axis=1)
            masked, hits = histogram_terms(codes, scaled, width)
            left[b].append(masked)
            right[b].append(hits)
    scale_ref[...] += scale
    for b in range(BOOKS):
        total_ref[b] += lax.dot_general(
            jnp.concatenate(left[b], axis=1),
            jnp.concatenate(right[b], axis=1),
            (((1,), (1,)), ((), ())),
            preferred_element_type=jnp.float32,
        )

    @pl.when(step == pl.num_programs(0) - 1)
    def _():
        shape = (GROUP, 8 * HIGH)
        column = lax.broadcasted_iota(jnp.int32, shape, 1) // HIGH
        for b in range(BOOKS):
            for v in range(LOW):
                part = jnp.zeros(shape, jnp.float32)
                for g in range(8):
                    block = total_ref[b, pl.ds((v * 8 + g) * GROUP, GROUP), :]
                    part = part + jnp.where(column == g, block, 0.0)
                book_ref[b, pl.ds(v * GROUP, GROUP), :] = part


def gradients(me, n, codes, x, pieces, weights, coef, after, first, width, span=(0, 1)):
    groups = codes.shape[1]
    blocks, features, tokens_block = x.shape
    tile_groups = largest_tile(groups, 32)
    tile = tile_groups * GROUP
    tokens = blocks * tokens_block
    tiles = groups // tile_groups
    start, end = [round(tiles * at) for at in span]
    unit = math.gcd(first, width)
    parts = width // unit
    places = [first // unit + p for p in range(parts)]
    once = pl.Buffered(1)
    out_specs = [
        pl.BlockSpec((BOOKS, LOW * GROUP, 8 * HIGH), lambda f: (0, 0, 0)),
        pl.BlockSpec((GROUP, width), lambda f: (0, 0)),
    ]
    out_shape = [
        jax.ShapeDtypeStruct((BOOKS, LOW * GROUP, 8 * HIGH), jnp.float32),
        jax.ShapeDtypeStruct((GROUP, width), jnp.float32),
    ]
    if len(pieces) > 1:
        out_specs.insert(0, pl.BlockSpec((tokens, width), lambda f: (0, 0), pipeline_mode=once))
        out_shape.insert(0, jax.ShapeDtypeStruct((tokens, width), jnp.bfloat16))
    result = pl.pallas_call(
        functools.partial(gradient_kernel, n, tile, width, blocks, len(pieces), parts),
        grid=(end - start,),
        in_specs=[
            pl.BlockSpec(memory_space=pltpu.SMEM),
            pl.BlockSpec((blocks, tile, tokens_block), lambda f: (0, start + f, 0)),
            pl.BlockSpec((tile, width), lambda f: (start + f, 0)),
            pl.BlockSpec(memory_space=pl.ANY),
        ]
        + [pl.BlockSpec((BOOKS, tile_groups, unit), lambda f, p=p: (0, start + f, p)) for p in places]
        + [pl.BlockSpec((1, unit), lambda f, p=p: (0, p)) for p in places]
        + [pl.BlockSpec(p.shape, lambda f: (0, 0), pipeline_mode=once) for p in pieces],
        out_specs=out_specs,
        out_shape=out_shape,
        scratch_shapes=[pltpu.VMEM((BOOKS, LOW * 8 * GROUP, 8 * HIGH), jnp.float32)],
        compiler_params=pltpu.CompilerParams(vmem_limit_bytes=VMEM),
        cost_estimate=pl.CostEstimate(
            flops=9 * tokens * features * width * (end - start) // tiles,
            bytes_accessed=2 * (tokens + 2 * features) * width * (end - start) // tiles,
            transcendentals=0,
        ),
        name="weight_gradients",
    )(me, x, weights, after, *([codes] * parts), *([coef] * parts), *pieces)
    return result if len(pieces) > 1 else [pieces[0], *result]


def input_gradient_kernel(count, refs):
    left = jnp.concatenate([refs[s][...] for s in range(count)], axis=1)
    right = jnp.concatenate([refs[count + s][...] for s in range(count)], axis=1)
    return lax.dot_general(left, right, (((1,), (1,)), ((), ())), preferred_element_type=jnp.float32)


def early_kernel(count, added, *refs):
    total = input_gradient_kernel(count, refs)
    refs[-1][...] = refs[2 * count][...] + total if added else total


def early_input_gradient(cots, weights, total, after):
    tokens, features = cots[0].shape[0], weights[0].shape[0]
    tile_t, tile_f = largest_tile(tokens, 512), largest_tile(features, 1024)
    width = sum(c.shape[1] for c in cots)
    out_spec = pl.BlockSpec((tile_t, tile_f), lambda f, t: (t, f))
    args = [*cots, *weights] + ([] if total is None else [total]) + [after]
    return pl.pallas_call(
        functools.partial(early_kernel, len(cots), total is not None),
        grid=(features // tile_f, tokens // tile_t),
        in_specs=[pl.BlockSpec((tile_t, c.shape[1]), lambda f, t: (t, 0)) for c in cots]
        + [pl.BlockSpec((tile_f, w.shape[1]), lambda f, t: (f, 0)) for w in weights]
        + ([] if total is None else [out_spec])
        + [pl.BlockSpec(memory_space=pl.ANY)],
        out_specs=out_spec,
        out_shape=jax.ShapeDtypeStruct((tokens, features), jnp.float32),
        input_output_aliases={} if total is None else {2 * len(cots): 0},
        compiler_params=pltpu.CompilerParams(vmem_limit_bytes=VMEM),
        cost_estimate=pl.CostEstimate(
            flops=3 * tokens * features * width,
            bytes_accessed=4 * tokens * features + 2 * (tokens + features) * width,
            transcendentals=0,
        ),
        name="early_input_gradient",
    )(*args)


def last_kernel(n, rows, block, fulls, count, me_ref, early_ref, *refs):
    cots, weights, refs = refs[:fulls], refs[fulls : 2 * fulls + 1], refs[2 * fulls + 1 :]
    pieces, (one_ref, two_ref, cot_ref) = refs[:count], refs[count:]

    @pl.when(pl.program_id(0) == 0)
    def _():
        place_pieces(me_ref[0], n, rows, pieces, cot_ref)

    start = pl.multiple_of((2 * pl.program_id(0) + me_ref[1]) * block, 16)
    left = jnp.concatenate([ref[...] for ref in cots] + [cot_ref[pl.ds(start, block), :]], axis=1)
    half = one_ref.shape[1]
    for out_ref, columns in ((one_ref, slice(0, half)), (two_ref, slice(half, 2 * half))):
        right = jnp.concatenate([ref[columns, :] for ref in weights], axis=1)
        part = lax.dot_general(left, right, (((1,), (1,)), ((), ())), preferred_element_type=jnp.float32)
        out_ref[...] = (early_ref[:, columns] + part).astype(out_ref.dtype)


def last_input_gradient(me, n, block, cots, pieces, weights, early, dtype):
    rows = pieces[0].shape[0]
    tokens, features = early.shape
    once = pl.Buffered(1)
    half = tokens // (2 * block)
    width = sum(w.shape[1] for w in weights)
    return pl.pallas_call(
        functools.partial(last_kernel, n, rows, block, len(cots), len(pieces)),
        grid_spec=pltpu.PrefetchScalarGridSpec(
            num_scalar_prefetch=1,
            grid=(half,),
            in_specs=[pl.BlockSpec((block, features), lambda t, who: (2 * t + who[1], 0))]
            + [pl.BlockSpec((block, c.shape[1]), lambda t, who: (2 * t + who[1], 0)) for c in cots]
            + [pl.BlockSpec(w.shape, lambda t, who: (0, 0), pipeline_mode=once) for w in weights]
            + [pl.BlockSpec(p.shape, lambda t, who: (0, 0), pipeline_mode=once) for p in pieces],
            out_specs=[pl.BlockSpec((block, features // 2), lambda t, who: (t, 0))] * 2,
            scratch_shapes=[pltpu.VMEM((tokens, pieces[0].shape[1]), jnp.bfloat16)],
        ),
        out_shape=[jax.ShapeDtypeStruct((tokens // 2, features // 2), dtype)] * 2,
        compiler_params=pltpu.CompilerParams(vmem_limit_bytes=VMEM),
        cost_estimate=pl.CostEstimate(
            flops=2 * tokens * features * width, bytes_accessed=3 * tokens * features, transcendentals=0
        ),
        name="last_input_gradient",
    )(me, early, *cots, *weights, *pieces)


class HalvingScatter:
    def __init__(self, terms, size):
        self.size = size
        self.me = lax.axis_index("dout")
        self.order = list(range(1, size.bit_length() - 1))
        self.step = 0
        rows = 2 * terms[0][0].shape[0] // size
        shape = (2,) * len(self.order) + (rows, terms[0][0].shape[1])
        self.terms = [[t.reshape(shape) for t in half] for half in terms]

    @staticmethod
    def total(terms):
        return sum((t.astype(jnp.float32) for t in terms[1:]), terms[0].astype(jnp.float32))

    def exchange(self, gate=None):
        gives, helds = [], []
        for which in range(2):
            axis, bit = self.place(which)
            mine = (self.me >> bit) & 1
            terms = self.terms[which]
            helds.append([lax.dynamic_index_in_dim(t, mine, axis, keepdims=False) for t in terms])
            give = self.total([lax.dynamic_index_in_dim(t, 1 - mine, axis, keepdims=False) for t in terms])
            gives.append(give.astype(jnp.bfloat16))
        if gate is not None:
            gives, gate = lax.optimization_barrier((gives, gate))
        for which in range(2):
            bit = self.place(which)[1]
            came = lax.ppermute(gives[which], "dout", [(a, a ^ (1 << bit)) for a in range(self.size)])
            self.terms[which] = helds[which] + [came]
        self.step += 1
        return gives if gate is None else gate

    def place(self, which):
        order = self.order if which == 0 else self.order[::-1]
        left = [b for b in reversed(self.order) if b not in order[: self.step]]
        return left.index(order[self.step]), order[self.step]

    def finish(self, gate):
        while self.step < len(self.order):
            gate = self.exchange(gate)
        return jnp.concatenate([self.total(t) for t in self.terms], axis=-1).astype(jnp.bfloat16), gate


def butterfly_sum(value, axis, size):
    if size & (size - 1):
        return lax.psum(value, axis)

    def other(bits):
        return lax.ppermute(value, axis, [(a, a ^ bits) for a in range(size)])

    bit = 1
    while bit < size:
        if 2 * bit < size:
            near, far, both = other(bit), other(2 * bit), other(3 * bit)
            value = (value + near) + (far + both)
            bit *= 4
        else:
            value = value + other(bit)
            bit *= 2
    return value


def local(n_din, n_dout, inputs, cotangent, codes, codebooks, scales, book_mean, book_var, scale_mean, scale_var):
    norm_factor = 1.0 / (2.0 * DOUT) ** 0.5
    loss_scale = (TOKENS * DIN / 4096.0) ** 0.5
    coef = scales * norm_factor
    outs = codes.shape[2]
    me = lax.axis_index("din").astype(jnp.int32).reshape(1)

    table, unit = packed_table(codebooks)
    coef_row = coef.reshape(1, outs)
    unit_row = coef_row * unit

    widths = split_columns(outs)
    firsts = [sum(widths[:i]) for i in range(len(widths))]
    final = len(widths) - 1
    owns = [lax.slice_in_dim(cotangent, f, f + w, axis=1) for f, w in zip(firsts, widths)]
    rings = [Ring(n_din, own.shape[0]) for own in owns]
    weights = [None] * len(widths)
    books, scale_parts, cots = [], [], []

    def run_decode(s, after):
        weights[s] = decode(codes, table, unit_row, after, firsts[s], widths[s])

    def run_gradients(s, after, span=(0, 1)):
        pieces = rings[s].pieces if span[0] == 0 else [cots[s]]
        cot, book, scale = gradients(
            me, n_din, codes, x, pieces, weights[s], coef_row, after, firsts[s], widths[s], span
        )
        if span[0] == 0:
            cots.append(cot)
            scale_parts.append(jnp.sum(scale, axis=0))
        else:
            scale_parts[s] += jnp.sum(scale, axis=0)
        books.append(book)
        return scale

    blocks, owns[0] = lax.optimization_barrier((inputs, owns[0]))
    if inputs.shape[0] % LANES == 0:
        x = lax.all_gather(transpose(blocks), "dout", axis=0, tiled=True)
        x = x.reshape(n_dout, inputs.shape[1], inputs.shape[0])
    else:
        x = lax.all_gather(blocks, "dout", axis=0, tiled=True).T[None]
    rings[0].begin(owns[0])
    run_decode(0, coef_row)
    if final > 0:
        run_decode(1, coef_row)
    early, summed, gate = None, 0, weights[min(1, final)]
    for s in range(final + 1):
        gate = rings[s].hold(gate)
        if s == 0:
            weights[min(1, final)] = gate
        rings[s].finish()
        if s == 0 and final >= 2:
            run_decode(2, gate)
            gate = weights[2]
        if 0 < s < final + 1:
            early = early_input_gradient(cots[summed:], weights[summed:s], early, gate)
            summed, gate = s, early
        if s < final:
            gate = rings[s].hold(gate)
            owns[s + 1], gate = lax.optimization_barrier((owns[s + 1], gate))
            if s > 0:
                early = gate
            elif final >= 2:
                weights[2] = gate
            rings[s + 1].begin(owns[s + 1])
            gate = run_gradients(s, gate)
            if s == 0:
                for later in range(3, final + 1):
                    run_decode(later, gate)
                    gate = weights[later]

    block = inputs.shape[0]
    if early is not None and n_dout > 1 and n_dout & (n_dout - 1) == 0:
        core = lax.axis_index("dout").astype(jnp.int32) & 1
        both_me = [jnp.stack([me[0], 1 - core]), jnp.stack([me[0], core])]
        pieces = rings[final].pieces
        rest = (n_din, block, cots[summed:], pieces, weights[summed:], early)
        give = last_input_gradient(both_me[0], *rest, jnp.bfloat16)
        got = [lax.ppermute(half, "dout", [(a, a ^ 1) for a in range(n_dout)]) for half in give]
        keep = last_input_gradient(both_me[1], *rest, jnp.float32)
        scatter = HalvingScatter([[k, g] for k, g in zip(keep, got)], n_dout)
        gate = keep[0]
        if n_dout > 2:
            gate = lax.optimization_barrier(scatter.exchange())[0]
        cut = 5 / 8 if codes.shape[1] >= 256 else 1
        gate = run_gradients(final, gate, (0, cut))
        grad_input, gate = scatter.finish(gate)
        if cut < 1:
            run_gradients(final, gate, (cut, 1))
        grad_input, books[-1] = lax.optimization_barrier((grad_input, books[-1]))
    else:
        run_gradients(final, gate)
        rows = early_input_gradient(cots, weights, None, gate)
        grad_input = lax.psum_scatter(rows, "dout", scatter_dimension=0, tiled=True).astype(jnp.bfloat16)

    book = sum(books[1:], books[0]).reshape(BOOKS, LOW, GROUP, 8, HIGH).sum(axis=3)
    book = book.transpose(0, 3, 1, 2).reshape(BOOKS * KCODE * GROUP)
    scale_total = jnp.concatenate(scale_parts) / coef
    both = butterfly_sum(jnp.concatenate([book, scale_total]), "din", n_din)
    grad_sums = butterfly_sum(both[: book.shape[0]], "dout", n_dout).reshape(BOOKS, KCODE, GROUP)
    scale_sums = both[book.shape[0] :]

    book_grad = grad_sums / loss_scale
    scale_grad = scale_sums * norm_factor / loss_scale
    new_books, new_book_mean, new_book_var = adam_step(codebooks, book_mean, book_var, book_grad)
    new_scales, new_scale_mean, new_scale_var = adam_step(scales, scale_mean, scale_var, scale_grad)
    return (
        grad_input,
        book_grad,
        new_books,
        new_book_mean,
        new_book_var,
        new_scales,
        new_scale_mean,
        new_scale_var,
    )


def solution(mesh):
    in_specs = (
        P("dout", "din"),
        P("din", "dout"),
        P(None, "din", "dout"),
        P(),
        P("dout"),
        P(),
        P(),
        P("dout"),
        P("dout"),
    )
    out_specs = (P("dout", "din"), P(), P(), P(), P(), P("dout"), P("dout"), P("dout"))
    body = functools.partial(local, mesh.shape["din"], mesh.shape["dout"])
    return jax.shard_map(body, mesh=mesh, in_specs=in_specs, out_specs=out_specs, check_vma=False)
```

```python
import functools
import math

import jax
import jax.numpy as jnp
from jax import lax
from jax.experimental import pallas as pl
from jax.experimental.pallas import tpu as pltpu
from jax.sharding import PartitionSpec as P

DIN = 8192
DOUT = 28672
KCODE = 256
BOOKS = 2
GROUP = 8
TOKENS = 2048

LANES = 128
LOW = 8
HIGH = KCODE // LOW
VMEM = 56 * 1024 * 1024

beta_one = 0.9
beta_two = 0.999
adam_rate = 0.01
adam_eps = 1e-08
corr_one = 1.0 - 0.9**10
corr_two = 1.0 - 0.999**10


def adam_step(param, mean_old, var_old, gradient):
    mean_new = beta_one * mean_old + (1.0 - beta_one) * gradient
    var_new = beta_two * var_old + (1.0 - beta_two) * gradient * gradient
    update = mean_new / corr_one / (jnp.sqrt(var_new / corr_two) + adam_eps)
    return (param - adam_rate * update, mean_new, var_new)


def split_columns(outs):
    unit = next((u for u in (2 * LANES,) if outs % u == 0), LANES)
    units = outs // unit
    shares = (5, 5, 4)
    ends = [round(units * sum(shares[: i + 1]) / sum(shares)) for i in range(len(shares))]
    widths = [(end - start) * unit for start, end in zip([0] + ends, ends)]
    return [width for width in widths if width]


def largest_tile(size, limit):
    for tile in range(min(size, limit), 0, -1):
        if size % tile == 0 and tile % 8 == 0:
            return tile
    return size


def packed_table(codebooks):
    rounded = codebooks.astype(jnp.bfloat16).astype(jnp.float32).transpose(0, 2, 1)
    unit = jnp.maximum(jnp.max(jnp.abs(rounded)), 1e-30) / 32767.0
    fixed = jnp.round(rounded / unit).astype(jnp.int32)
    return fixed[..., :LANES] * 65536 + (fixed[..., LANES:] & 65535), unit


def decode_kernel(tile_groups, width, codes_ref, table_ref, coef_ref, _, weight_ref):
    @pl.loop(0, tile_groups // 8)
    def _(i):
        start = pl.multiple_of(i * 8, 8)
        for q in range(width // LANES):
            cols = pl.ds(q * LANES, LANES)
            code = [codes_ref[b, pl.ds(start, 8), cols] for b in range(BOOKS)]
            coef = jnp.broadcast_to(coef_ref[:, cols], (8, LANES))
            rows = []
            for g in range(8):
                total = None
                for b in range(BOOKS):
                    c = jnp.broadcast_to(code[b][g : g + 1], (8, LANES))
                    word = jnp.take_along_axis(table_ref[b], c & (LANES - 1), axis=1, mode="promise_in_bounds")
                    value = (word << ((c & LANES) >> 3)) >> 16
                    total = value if total is None else total + value
                rows.append(total.astype(jnp.float32) * coef)
            weight_ref[pl.ds(pl.multiple_of(i * 64, 64), 64), cols] = jnp.concatenate(
                rows, axis=0
            ).astype(jnp.bfloat16)


def decode(codes, table, coef, after, first, width):
    groups = codes.shape[1]
    tile_groups = largest_tile(groups, 64)
    unit = math.gcd(first, width)
    if unit > 12 * LANES:
        unit = math.gcd(unit, 4 * LANES)
    return pl.pallas_call(
        functools.partial(decode_kernel, tile_groups, unit),
        grid=(width // unit, groups // tile_groups),
        in_specs=[
            pl.BlockSpec((BOOKS, tile_groups, unit), lambda o, f: (0, f, first // unit + o)),
            pl.BlockSpec(table.shape, lambda o, f: (0, 0, 0)),
            pl.BlockSpec((1, unit), lambda o, f: (0, first // unit + o)),
            pl.BlockSpec(memory_space=pl.ANY),
        ],
        out_specs=pl.BlockSpec((tile_groups * GROUP, unit), lambda o, f: (f, o)),
        out_shape=jax.ShapeDtypeStruct((groups * GROUP, width), jnp.bfloat16),
        compiler_params=pltpu.CompilerParams(vmem_limit_bytes=VMEM),
        cost_estimate=pl.CostEstimate(
            flops=groups * GROUP * width * 9000, bytes_accessed=groups * width * 24, transcendentals=0
        ),
        name="decode_weights",
    )(codes, table, coef, after)


def piece_places(n, rows):
    places = []
    for d in range(1, (n - 1) // 2 + 1):
        places += [(-d, 0, rows), (d, 0, rows)]
    if n % 2 == 0:
        places += [(-(n // 2), 0, rows)]
    return places


class Ring:
    def __init__(self, n, rows):
        self.n, self.rows = n, rows
        self.forward = [(a, (a + 1) % n) for a in range(n)]
        self.backward = [((a + 1) % n, a) for a in range(n)]

    def begin(self, own):
        self.pieces = [own]
        self.left = self.right = own
        for _ in range(1, (self.n - 1) // 2 + 1):
            self.left = lax.ppermute(self.left, "din", self.forward)
            self.right = lax.ppermute(self.right, "din", self.backward)
            self.pieces += [self.left, self.right]

    def hold(self, gate):
        first = len(self.pieces) > 1
        held, gate = lax.optimization_barrier((self.pieces, gate))
        self.pieces = list(held)
        if first:
            self.left = self.pieces[-2]
        return gate

    def finish(self):
        if self.n % 2 == 0:
            self.pieces.append(lax.ppermute(self.left, "din", self.forward))


def transpose_kernel(in_ref, out_ref):
    out_ref[...] = in_ref[...].T


def transpose(block):
    rows, columns = block.shape
    tile = largest_tile(columns, 512)
    return pl.pallas_call(
        transpose_kernel,
        grid=(columns // tile,),
        in_specs=[pl.BlockSpec((rows, tile), lambda c: (0, c))],
        out_specs=pl.BlockSpec((tile, rows), lambda c: (c, 0)),
        out_shape=jax.ShapeDtypeStruct((columns, rows), block.dtype),
        name="transpose_inputs",
    )(block)


def place_pieces(me, n, rows, pieces, out_ref):
    for piece, (shift, skip, count) in zip(pieces, [(0, 0, rows)] + piece_places(n, rows)):
        chunk = lax.rem(me + shift + 2 * n, n)
        out_ref[pl.ds(pl.multiple_of(chunk * rows + skip, 16), count), :] = piece[...]


def histogram_terms(codes, scaled, width):
    spread = jnp.broadcast_to(codes[:, None, :], (8, GROUP, width)).reshape(8 * GROUP, width)
    low = (spread & (LOW - 1)).astype(jnp.bfloat16)
    zero = jnp.bfloat16(0)
    left = jnp.concatenate([jnp.where(low == jnp.bfloat16(v), scaled, zero) for v in range(LOW)], axis=0)
    iota = lax.broadcasted_iota(jnp.int32, (HIGH, width), 0).astype(jnp.bfloat16)
    hits = []
    for g in range(8):
        high = jnp.broadcast_to(codes[g : g + 1] >> 3, (16, width)).astype(jnp.bfloat16)
        for m in range(HIGH // 16):
            hits.append(jnp.where(high == iota[m * 16 : (m + 1) * 16], jnp.bfloat16(1), zero))
    return left, jnp.concatenate(hits, axis=0)


def gradient_kernel(n, tile, width, blocks, count, parts, me_ref, x_ref, weight_ref, _, *refs):
    code_refs, coef_refs, refs = refs[:parts], refs[parts : 2 * parts], refs[2 * parts :]
    pieces, refs = refs[:count], refs[count:]
    cot_ref = refs[0] if count > 1 else pieces[0]
    book_ref, scale_ref, total_ref = refs[-3:]
    step = pl.program_id(0)

    @pl.when(step == 0)
    def _():
        total_ref[...] = jnp.zeros_like(total_ref)
        scale_ref[...] = jnp.zeros_like(scale_ref)
        if count > 1:
            place_pieces(me_ref[0], n, pieces[0].shape[0], pieces, cot_ref)

    x = jnp.concatenate([x_ref[e] for e in range(blocks)], axis=1) if blocks > 1 else x_ref[0]
    grads = jnp.dot(x, cot_ref[...], preferred_element_type=jnp.float32)
    coef = jnp.concatenate([ref[...] for ref in coef_refs], axis=1)
    scale = jnp.zeros((GROUP, width), jnp.float32)
    left, right = [[] for _ in range(BOOKS)], [[] for _ in range(BOOKS)]
    for i in range(tile // 64):
        grad = grads[i * 64 : (i + 1) * 64]
        scaled = (grad * coef).astype(jnp.bfloat16)
        product = grad * weight_ref[i * 64 : (i + 1) * 64, :].astype(jnp.float32)
        scale = scale + jnp.sum(product.reshape(8, GROUP, width), axis=0)
        for b in range(BOOKS):
            codes = jnp.concatenate([ref[b, i * 8 : (i + 1) * 8, :] for ref in code_refs], axis=1)
            masked, hits = histogram_terms(codes, scaled, width)
            left[b].append(masked)
            right[b].append(hits)
    scale_ref[...] += scale
    for b in range(BOOKS):
        total_ref[b] += lax.dot_general(
            jnp.concatenate(left[b], axis=1),
            jnp.concatenate(right[b], axis=1),
            (((1,), (1,)), ((), ())),
            preferred_element_type=jnp.float32,
        )

    @pl.when(step == pl.num_programs(0) - 1)
    def _():
        shape = (GROUP, 8 * HIGH)
        column = lax.broadcasted_iota(jnp.int32, shape, 1) // HIGH
        for b in range(BOOKS):
            for v in range(LOW):
                part = jnp.zeros(shape, jnp.float32)
                for g in range(8):
                    block = total_ref[b, pl.ds((v * 8 + g) * GROUP, GROUP), :]
                    part = part + jnp.where(column == g, block, 0.0)
                book_ref[b, pl.ds(v * GROUP, GROUP), :] = part


def gradients(me, n, codes, x, pieces, weights, coef, after, first, width, span=(0, 1)):
    groups = codes.shape[1]
    blocks, features, tokens_block = x.shape
    tile_groups = largest_tile(groups, 32)
    tile = tile_groups * GROUP
    tokens = blocks * tokens_block
    tiles = groups // tile_groups
    start, end = [round(tiles * at) for at in span]
    unit = math.gcd(first, width)
    parts = width // unit
    places = [first // unit + p for p in range(parts)]
    once = pl.Buffered(1)
    out_specs = [
        pl.BlockSpec((BOOKS, LOW * GROUP, 8 * HIGH), lambda f: (0, 0, 0)),
        pl.BlockSpec((GROUP, width), lambda f: (0, 0)),
    ]
    out_shape = [
        jax.ShapeDtypeStruct((BOOKS, LOW * GROUP, 8 * HIGH), jnp.float32),
        jax.ShapeDtypeStruct((GROUP, width), jnp.float32),
    ]
    if len(pieces) > 1:
        out_specs.insert(0, pl.BlockSpec((tokens, width), lambda f: (0, 0), pipeline_mode=once))
        out_shape.insert(0, jax.ShapeDtypeStruct((tokens, width), jnp.bfloat16))
    result = pl.pallas_call(
        functools.partial(gradient_kernel, n, tile, width, blocks, len(pieces), parts),
        grid=(end - start,),
        in_specs=[
            pl.BlockSpec(memory_space=pltpu.SMEM),
            pl.BlockSpec((blocks, tile, tokens_block), lambda f: (0, start + f, 0)),
            pl.BlockSpec((tile, width), lambda f: (start + f, 0)),
            pl.BlockSpec(memory_space=pl.ANY),
        ]
        + [pl.BlockSpec((BOOKS, tile_groups, unit), lambda f, p=p: (0, start + f, p)) for p in places]
        + [pl.BlockSpec((1, unit), lambda f, p=p: (0, p)) for p in places]
        + [pl.BlockSpec(p.shape, lambda f: (0, 0), pipeline_mode=once) for p in pieces],
        out_specs=out_specs,
        out_shape=out_shape,
        scratch_shapes=[pltpu.VMEM((BOOKS, LOW * 8 * GROUP, 8 * HIGH), jnp.float32)],
        compiler_params=pltpu.CompilerParams(vmem_limit_bytes=VMEM),
        cost_estimate=pl.CostEstimate(
            flops=9 * tokens * features * width * (end - start) // tiles,
            bytes_accessed=2 * (tokens + 2 * features) * width * (end - start) // tiles,
            transcendentals=0,
        ),
        name="weight_gradients",
    )(me, x, weights, after, *([codes] * parts), *([coef] * parts), *pieces)
    return result if len(pieces) > 1 else [pieces[0], *result]


def input_gradient_kernel(count, refs):
    left = jnp.concatenate([refs[s][...] for s in range(count)], axis=1)
    right = jnp.concatenate([refs[count + s][...] for s in range(count)], axis=1)
    return lax.dot_general(left, right, (((1,), (1,)), ((), ())), preferred_element_type=jnp.float32)


def early_kernel(count, added, *refs):
    total = input_gradient_kernel(count, refs)
    refs[-1][...] = refs[2 * count][...] + total if added else total


def early_input_gradient(cots, weights, total, after):
    tokens, features = cots[0].shape[0], weights[0].shape[0]
    tile_t, tile_f = largest_tile(tokens, 512), largest_tile(features, 1024)
    width = sum(c.shape[1] for c in cots)
    out_spec = pl.BlockSpec((tile_t, tile_f), lambda f, t: (t, f))
    args = [*cots, *weights] + ([] if total is None else [total]) + [after]
    return pl.pallas_call(
        functools.partial(early_kernel, len(cots), total is not None),
        grid=(features // tile_f, tokens // tile_t),
        in_specs=[pl.BlockSpec((tile_t, c.shape[1]), lambda f, t: (t, 0)) for c in cots]
        + [pl.BlockSpec((tile_f, w.shape[1]), lambda f, t: (f, 0)) for w in weights]
        + ([] if total is None else [out_spec])
        + [pl.BlockSpec(memory_space=pl.ANY)],
        out_specs=out_spec,
        out_shape=jax.ShapeDtypeStruct((tokens, features), jnp.float32),
        input_output_aliases={} if total is None else {2 * len(cots): 0},
        compiler_params=pltpu.CompilerParams(vmem_limit_bytes=VMEM),
        cost_estimate=pl.CostEstimate(
            flops=3 * tokens * features * width,
            bytes_accessed=4 * tokens * features + 2 * (tokens + features) * width,
            transcendentals=0,
        ),
        name="early_input_gradient",
    )(*args)


def last_kernel(n, rows, count, me_ref, early_ref, weight_ref, *refs):
    pieces, (one_ref, two_ref, cot_ref) = refs[:count], refs[count:]
    step, half = pl.program_id(0), pl.num_programs(0) // 2
    width = cot_ref.shape[1]

    @pl.when(step == 0)
    def _():
        for piece, (shift, _, _) in zip(pieces, [(0, 0, rows)] + piece_places(n, rows)):
            chunk = lax.rem(me_ref[0] + shift + 2 * n, n)
            start = pl.multiple_of(chunk * (rows // 2), 16)
            cot_ref[pl.ds(start, rows // 2), :] = piece[...].reshape(rows // 2, width)

    part = lax.dot_general(cot_ref[...], weight_ref[...], (((1,), (1,)), ((), ())), preferred_element_type=jnp.float32)
    total = (early_ref[...].reshape(part.shape) + part).astype(one_ref.dtype)

    @pl.when(step < half)
    def _():
        one_ref[...] = total

    @pl.when(step >= half)
    def _():
        two_ref[...] = total


def last_input_gradient(me, n, block, pieces, weights, early, dtype):
    rows, width = pieces[0].shape
    tokens, features = early.shape
    once = pl.Buffered(1)
    tile = largest_tile(features // 2, 512)
    half = features // 2 // tile
    pairs = rows // (2 * block)
    return pl.pallas_call(
        functools.partial(last_kernel, n, rows, len(pieces)),
        grid_spec=pltpu.PrefetchScalarGridSpec(
            num_scalar_prefetch=1,
            grid=(2 * half,),
            in_specs=[
                pl.BlockSpec((tokens // (2 * block), 1, block, tile), lambda f, who: (0, who[1], 0, f)),
                pl.BlockSpec((tile, width), lambda f, who: (f, 0)),
            ]
            + [pl.BlockSpec((pairs, 1, block, width), lambda f, who: (0, who[1], 0, 0), pipeline_mode=once) for _ in pieces],
            out_specs=[
                pl.BlockSpec((tokens // 2, tile), lambda f, who: (0, jnp.minimum(f, half - 1))),
                pl.BlockSpec((tokens // 2, tile), lambda f, who: (0, jnp.maximum(f - half, 0))),
            ],
            scratch_shapes=[pltpu.VMEM((tokens // 2, width), jnp.bfloat16)],
        ),
        out_shape=[jax.ShapeDtypeStruct((tokens // 2, features // 2), dtype)] * 2,
        compiler_params=pltpu.CompilerParams(vmem_limit_bytes=VMEM),
        cost_estimate=pl.CostEstimate(
            flops=2 * tokens * features * width, bytes_accessed=3 * tokens * features, transcendentals=0
        ),
        name="last_input_gradient",
    )(
        me,
        early.reshape(tokens // (2 * block), 2, block, features),
        weights,
        *[piece.reshape(pairs, 2, block, width) for piece in pieces],
    )


class HalvingScatter:
    def __init__(self, terms, size):
        self.size = size
        self.me = lax.axis_index("dout")
        self.order = list(range(1, size.bit_length() - 1))
        self.step = 0
        rows = 2 * terms[0][0].shape[0] // size
        shape = (2,) * len(self.order) + (rows, terms[0][0].shape[1])
        self.terms = [[t.reshape(shape) for t in half] for half in terms]

    @staticmethod
    def total(terms):
        return sum((t.astype(jnp.float32) for t in terms[1:]), terms[0].astype(jnp.float32))

    def exchange(self, gate=None):
        gives, helds = [], []
        for which in range(2):
            axis, bit = self.place(which)
            mine = (self.me >> bit) & 1
            terms = self.terms[which]
            helds.append([lax.dynamic_index_in_dim(t, mine, axis, keepdims=False) for t in terms])
            give = self.total([lax.dynamic_index_in_dim(t, 1 - mine, axis, keepdims=False) for t in terms])
            gives.append(give.astype(jnp.bfloat16))
        if gate is not None:
            gives, gate = lax.optimization_barrier((gives, gate))
        for which in range(2):
            bit = self.place(which)[1]
            came = lax.ppermute(gives[which], "dout", [(a, a ^ (1 << bit)) for a in range(self.size)])
            self.terms[which] = helds[which] + [came]
        self.step += 1
        return gives if gate is None else gate

    def place(self, which):
        order = self.order if which == 0 else self.order[::-1]
        left = [b for b in reversed(self.order) if b not in order[: self.step]]
        return left.index(order[self.step]), order[self.step]

    def hold(self, gate):
        came, gate = lax.optimization_barrier(([terms[-1] for terms in self.terms], gate))
        self.terms = [[*terms[:-1], new] for terms, new in zip(self.terms, came)]
        return gate

    def finish(self):
        return jnp.concatenate([self.total(t) for t in self.terms], axis=-1).astype(jnp.bfloat16)


def butterfly_sum(value, axis, size):
    if size & (size - 1):
        return lax.psum(value, axis)

    def other(bits):
        return lax.ppermute(value, axis, [(a, a ^ bits) for a in range(size)])

    bit = 1
    while bit < size:
        if 2 * bit < size:
            near, far, both = other(bit), other(2 * bit), other(3 * bit)
            value = (value + near) + (far + both)
            bit *= 4
        else:
            value = value + other(bit)
            bit *= 2
    return value


def local(n_din, n_dout, inputs, cotangent, codes, codebooks, scales, book_mean, book_var, scale_mean, scale_var):
    norm_factor = 1.0 / (2.0 * DOUT) ** 0.5
    loss_scale = (TOKENS * DIN / 4096.0) ** 0.5
    coef = scales * norm_factor
    outs = codes.shape[2]
    me = lax.axis_index("din").astype(jnp.int32).reshape(1)

    table, unit = packed_table(codebooks)
    coef_row = coef.reshape(1, outs)
    unit_row = coef_row * unit

    widths = split_columns(outs)
    firsts = [sum(widths[:i]) for i in range(len(widths))]
    final = len(widths) - 1
    owns = [lax.slice_in_dim(cotangent, f, f + w, axis=1) for f, w in zip(firsts, widths)]
    rings = [Ring(n_din, own.shape[0]) for own in owns]
    weights = [None] * len(widths)
    books, scale_parts, cots = [], [], []

    def run_decode(s, after):
        weights[s] = decode(codes, table, unit_row, after, firsts[s], widths[s])

    def run_gradients(s, after, span=(0, 1)):
        pieces = rings[s].pieces if span[0] == 0 else [cots[s]]
        cot, book, scale = gradients(
            me, n_din, codes, x, pieces, weights[s], coef_row, after, firsts[s], widths[s], span
        )
        if span[0] == 0:
            cots.append(cot)
            scale_parts.append(jnp.sum(scale, axis=0))
        else:
            scale_parts[s] += jnp.sum(scale, axis=0)
        books.append(book)
        return scale

    blocks, owns[0] = lax.optimization_barrier((inputs, owns[0]))
    if inputs.shape[0] % LANES == 0:
        x = lax.all_gather(transpose(blocks), "dout", axis=0, tiled=True)
        x = x.reshape(n_dout, inputs.shape[1], inputs.shape[0])
    else:
        x = lax.all_gather(blocks, "dout", axis=0, tiled=True).T[None]
    rings[0].begin(owns[0])
    run_decode(0, coef_row)
    if final > 0:
        run_decode(1, coef_row)
    early, summed, gate = None, 0, weights[min(1, final)]
    for s in range(final + 1):
        gate = rings[s].hold(gate)
        if s == 0:
            weights[min(1, final)] = gate
        rings[s].finish()
        if s == 0 and final >= 2:
            run_decode(2, gate)
            gate = weights[2]
        if 0 < s < final + 1:
            early = early_input_gradient(cots[summed:], weights[summed:s], early, gate)
            summed, gate = s, early
        if s < final:
            gate = rings[s].hold(gate)
            owns[s + 1], gate = lax.optimization_barrier((owns[s + 1], gate))
            if s > 0:
                early = gate
            elif final >= 2:
                weights[2] = gate
            rings[s + 1].begin(owns[s + 1])
            gate = run_gradients(s, gate)
            if s == 0:
                for later in range(3, final + 1):
                    run_decode(later, gate)
                    gate = weights[later]

    block = inputs.shape[0]
    if early is not None and n_dout > 1 and n_dout & (n_dout - 1) == 0 and owns[0].shape[0] % (2 * block) == 0:
        core = lax.axis_index("dout").astype(jnp.int32) & 1
        both_me = [jnp.stack([me[0], 1 - core]), jnp.stack([me[0], core])]
        pieces = rings[final].pieces
        rest = (n_din, block, pieces, weights[final], early)
        give = last_input_gradient(both_me[0], *rest, jnp.bfloat16)
        got = [lax.ppermute(half, "dout", [(a, a ^ 1) for a in range(n_dout)]) for half in give]
        keep = last_input_gradient(both_me[1], *rest, jnp.float32)
        scatter = HalvingScatter([[k, g] for k, g in zip(keep, got)], n_dout)
        gate = keep[0]
        if n_dout > 2:
            gate = lax.optimization_barrier(scatter.exchange())[0]
        cut = 5 / 8 if codes.shape[1] >= 256 else 1
        gate = run_gradients(final, gate, (0, cut))
        while scatter.step < len(scatter.order):
            gate = scatter.exchange(gate)
        if cut < 1:
            run_gradients(final, gate, (cut, 1))
            books[-1] = scatter.hold(books[-1])
        grad_input = scatter.finish()
    else:
        run_gradients(final, gate)
        rows = early_input_gradient(cots, weights, None, gate)
        grad_input = lax.psum_scatter(rows, "dout", scatter_dimension=0, tiled=True).astype(jnp.bfloat16)

    book = sum(books[1:], books[0]).reshape(BOOKS, LOW, GROUP, 8, HIGH).sum(axis=3)
    book = book.transpose(0, 3, 1, 2).reshape(BOOKS * KCODE * GROUP)
    scale_total = jnp.concatenate(scale_parts) / coef
    both = butterfly_sum(jnp.concatenate([book, scale_total]), "din", n_din)
    grad_sums = butterfly_sum(both[: book.shape[0]], "dout", n_dout).reshape(BOOKS, KCODE, GROUP)
    scale_sums = both[book.shape[0] :]

    book_grad = grad_sums / loss_scale
    scale_grad = scale_sums * norm_factor / loss_scale
    new_books, new_book_mean, new_book_var = adam_step(codebooks, book_mean, book_var, book_grad)
    new_scales, new_scale_mean, new_scale_var = adam_step(scales, scale_mean, scale_var, scale_grad)
    return (
        grad_input,
        book_grad,
        new_books,
        new_book_mean,
        new_book_var,
        new_scales,
        new_scale_mean,
        new_scale_var,
    )


def solution(mesh):
    in_specs = (
        P("dout", "din"),
        P("din", "dout"),
        P(None, "din", "dout"),
        P(),
        P("dout"),
        P(),
        P(),
        P("dout"),
        P("dout"),
    )
    out_specs = (P("dout", "din"), P(), P(), P(), P(), P("dout"), P("dout"), P("dout"))
    body = functools.partial(local, mesh.shape["din"], mesh.shape["dout"])
    return jax.shard_map(body, mesh=mesh, in_specs=in_specs, out_specs=out_specs, check_vma=False)
```

```python
import functools
import math

import jax
import jax.numpy as jnp
from jax import lax
from jax.experimental import pallas as pl
from jax.experimental.pallas import tpu as pltpu
from jax.sharding import PartitionSpec as P

DIN = 8192
DOUT = 28672
KCODE = 256
BOOKS = 2
GROUP = 8
TOKENS = 2048

LANES = 128
LOW = 8
HIGH = KCODE // LOW
VMEM = 56 * 1024 * 1024

beta_one = 0.9
beta_two = 0.999
adam_rate = 0.01
adam_eps = 1e-08
corr_one = 1.0 - 0.9**10
corr_two = 1.0 - 0.999**10


def adam_step(param, mean_old, var_old, gradient):
    mean_new = beta_one * mean_old + (1.0 - beta_one) * gradient
    var_new = beta_two * var_old + (1.0 - beta_two) * gradient * gradient
    update = mean_new / corr_one / (jnp.sqrt(var_new / corr_two) + adam_eps)
    return (param - adam_rate * update, mean_new, var_new)


def split_columns(outs):
    unit = next((u for u in (2 * LANES,) if outs % u == 0), LANES)
    units = outs // unit
    shares = (5, 5, 4)
    ends = [round(units * sum(shares[: i + 1]) / sum(shares)) for i in range(len(shares))]
    widths = [(end - start) * unit for start, end in zip([0] + ends, ends)]
    return [width for width in widths if width]


def largest_tile(size, limit):
    for tile in range(min(size, limit), 0, -1):
        if size % tile == 0 and tile % 8 == 0:
            return tile
    return size


def packed_table(codebooks):
    rounded = codebooks.astype(jnp.bfloat16).astype(jnp.float32).transpose(0, 2, 1)
    unit = jnp.maximum(jnp.max(jnp.abs(rounded)), 1e-30) / 32767.0
    fixed = jnp.round(rounded / unit).astype(jnp.int32)
    return fixed[..., :LANES] * 65536 + (fixed[..., LANES:] & 65535), unit


def decode_kernel(tile_groups, width, codes_ref, table_ref, coef_ref, _, weight_ref):
    @pl.loop(0, tile_groups // 8)
    def _(i):
        start = pl.multiple_of(i * 8, 8)
        for q in range(width // LANES):
            cols = pl.ds(q * LANES, LANES)
            code = [codes_ref[b, pl.ds(start, 8), cols] for b in range(BOOKS)]
            coef = jnp.broadcast_to(coef_ref[:, cols], (8, LANES))
            rows = []
            for g in range(8):
                total = None
                for b in range(BOOKS):
                    c = jnp.broadcast_to(code[b][g : g + 1], (8, LANES))
                    word = jnp.take_along_axis(table_ref[b], c & (LANES - 1), axis=1, mode="promise_in_bounds")
                    value = (word << ((c & LANES) >> 3)) >> 16
                    total = value if total is None else total + value
                rows.append(total.astype(jnp.float32) * coef)
            weight_ref[pl.ds(pl.multiple_of(i * 64, 64), 64), cols] = jnp.concatenate(
                rows, axis=0
            ).astype(jnp.bfloat16)


def decode(codes, table, coef, after, first, width):
    groups = codes.shape[1]
    tile_groups = largest_tile(groups, 64)
    unit = math.gcd(first, width)
    if unit > 12 * LANES:
        unit = math.gcd(unit, 4 * LANES)
    return pl.pallas_call(
        functools.partial(decode_kernel, tile_groups, unit),
        grid=(width // unit, groups // tile_groups),
        in_specs=[
            pl.BlockSpec((BOOKS, tile_groups, unit), lambda o, f: (0, f, first // unit + o)),
            pl.BlockSpec(table.shape, lambda o, f: (0, 0, 0)),
            pl.BlockSpec((1, unit), lambda o, f: (0, first // unit + o)),
            pl.BlockSpec(memory_space=pl.ANY),
        ],
        out_specs=pl.BlockSpec((tile_groups * GROUP, unit), lambda o, f: (f, o)),
        out_shape=jax.ShapeDtypeStruct((groups * GROUP, width), jnp.bfloat16),
        compiler_params=pltpu.CompilerParams(vmem_limit_bytes=VMEM),
        cost_estimate=pl.CostEstimate(
            flops=groups * GROUP * width * 9000, bytes_accessed=groups * width * 24, transcendentals=0
        ),
        name="decode_weights",
    )(codes, table, coef, after)


def piece_places(n, rows):
    places = []
    for d in range(1, (n - 1) // 2 + 1):
        places += [(-d, 0, rows), (d, 0, rows)]
    if n % 2 == 0:
        places += [(-(n // 2), 0, rows)]
    return places


class Ring:
    def __init__(self, n, rows):
        self.n, self.rows = n, rows
        self.forward = [(a, (a + 1) % n) for a in range(n)]
        self.backward = [((a + 1) % n, a) for a in range(n)]

    def begin(self, own):
        self.pieces = [own]
        self.left = self.right = own
        for _ in range(1, (self.n - 1) // 2 + 1):
            self.left = lax.ppermute(self.left, "din", self.forward)
            self.right = lax.ppermute(self.right, "din", self.backward)
            self.pieces += [self.left, self.right]

    def hold(self, gate):
        first = len(self.pieces) > 1
        held, gate = lax.optimization_barrier((self.pieces, gate))
        self.pieces = list(held)
        if first:
            self.left = self.pieces[-2]
        return gate

    def finish(self):
        if self.n % 2 == 0:
            self.pieces.append(lax.ppermute(self.left, "din", self.forward))


def transpose_kernel(in_ref, out_ref):
    out_ref[...] = in_ref[...].T


def transpose(block):
    rows, columns = block.shape
    tile = largest_tile(columns, 512)
    return pl.pallas_call(
        transpose_kernel,
        grid=(columns // tile,),
        in_specs=[pl.BlockSpec((rows, tile), lambda c: (0, c))],
        out_specs=pl.BlockSpec((tile, rows), lambda c: (c, 0)),
        out_shape=jax.ShapeDtypeStruct((columns, rows), block.dtype),
        name="transpose_inputs",
    )(block)


def place_pieces(me, n, rows, pieces, out_ref):
    for piece, (shift, skip, count) in zip(pieces, [(0, 0, rows)] + piece_places(n, rows)):
        chunk = lax.rem(me + shift + 2 * n, n)
        out_ref[pl.ds(pl.multiple_of(chunk * rows + skip, 16), count), :] = piece[...]


def histogram_terms(codes, scaled, width):
    spread = jnp.broadcast_to(codes[:, None, :], (8, GROUP, width)).reshape(8 * GROUP, width)
    low = (spread & (LOW - 1)).astype(jnp.bfloat16)
    zero = jnp.bfloat16(0)
    left = jnp.concatenate([jnp.where(low == jnp.bfloat16(v), scaled, zero) for v in range(LOW)], axis=0)
    iota = lax.broadcasted_iota(jnp.int32, (HIGH, width), 0).astype(jnp.bfloat16)
    hits = []
    for g in range(8):
        high = jnp.broadcast_to(codes[g : g + 1] >> 3, (16, width)).astype(jnp.bfloat16)
        for m in range(HIGH // 16):
            hits.append(jnp.where(high == iota[m * 16 : (m + 1) * 16], jnp.bfloat16(1), zero))
    return left, jnp.concatenate(hits, axis=0)


def gradient_kernel(n, tile, width, blocks, count, parts, me_ref, x_ref, weight_ref, _, *refs):
    code_refs, coef_refs, refs = refs[:parts], refs[parts : 2 * parts], refs[2 * parts :]
    pieces, refs = refs[:count], refs[count:]
    cot_ref = refs[0] if count > 1 else pieces[0]
    book_ref, scale_ref, total_ref = refs[-3:]
    step = pl.program_id(0)

    @pl.when(step == 0)
    def _():
        total_ref[...] = jnp.zeros_like(total_ref)
        scale_ref[...] = jnp.zeros_like(scale_ref)
        if count > 1:
            place_pieces(me_ref[0], n, pieces[0].shape[0], pieces, cot_ref)

    x = jnp.concatenate([x_ref[e] for e in range(blocks)], axis=1) if blocks > 1 else x_ref[0]
    grads = jnp.dot(x, cot_ref[...], preferred_element_type=jnp.float32)
    coef = jnp.concatenate([ref[...] for ref in coef_refs], axis=1)
    scale = jnp.zeros((GROUP, width), jnp.float32)
    left, right = [[] for _ in range(BOOKS)], [[] for _ in range(BOOKS)]
    for i in range(tile // 64):
        grad = grads[i * 64 : (i + 1) * 64]
        scaled = (grad * coef).astype(jnp.bfloat16)
        product = grad * weight_ref[i * 64 : (i + 1) * 64, :].astype(jnp.float32)
        scale = scale + jnp.sum(product.reshape(8, GROUP, width), axis=0)
        for b in range(BOOKS):
            codes = jnp.concatenate([ref[b, i * 8 : (i + 1) * 8, :] for ref in code_refs], axis=1)
            masked, hits = histogram_terms(codes, scaled, width)
            left[b].append(masked)
            right[b].append(hits)
    scale_ref[...] += scale
    for b in range(BOOKS):
        total_ref[b] += lax.dot_general(
            jnp.concatenate(left[b], axis=1),
            jnp.concatenate(right[b], axis=1),
            (((1,), (1,)), ((), ())),
            preferred_element_type=jnp.float32,
        )

    @pl.when(step == pl.num_programs(0) - 1)
    def _():
        shape = (GROUP, 8 * HIGH)
        column = lax.broadcasted_iota(jnp.int32, shape, 1) // HIGH
        for b in range(BOOKS):
            for v in range(LOW):
                part = jnp.zeros(shape, jnp.float32)
                for g in range(8):
                    block = total_ref[b, pl.ds((v * 8 + g) * GROUP, GROUP), :]
                    part = part + jnp.where(column == g, block, 0.0)
                book_ref[b, pl.ds(v * GROUP, GROUP), :] = part


def gradients(me, n, codes, x, pieces, weights, coef, after, first, width, span=(0, 1)):
    groups = codes.shape[1]
    blocks, features, tokens_block = x.shape
    tile_groups = largest_tile(groups, 32)
    tile = tile_groups * GROUP
    tokens = blocks * tokens_block
    tiles = groups // tile_groups
    start, end = [round(tiles * at) for at in span]
    unit = math.gcd(first, width)
    parts = width // unit
    places = [first // unit + p for p in range(parts)]
    once = pl.Buffered(1)
    out_specs = [
        pl.BlockSpec((BOOKS, LOW * GROUP, 8 * HIGH), lambda f: (0, 0, 0)),
        pl.BlockSpec((GROUP, width), lambda f: (0, 0)),
    ]
    out_shape = [
        jax.ShapeDtypeStruct((BOOKS, LOW * GROUP, 8 * HIGH), jnp.float32),
        jax.ShapeDtypeStruct((GROUP, width), jnp.float32),
    ]
    if len(pieces) > 1:
        out_specs.insert(0, pl.BlockSpec((tokens, width), lambda f: (0, 0), pipeline_mode=once))
        out_shape.insert(0, jax.ShapeDtypeStruct((tokens, width), jnp.bfloat16))
    result = pl.pallas_call(
        functools.partial(gradient_kernel, n, tile, width, blocks, len(pieces), parts),
        grid=(end - start,),
        in_specs=[
            pl.BlockSpec(memory_space=pltpu.SMEM),
            pl.BlockSpec((blocks, tile, tokens_block), lambda f: (0, start + f, 0)),
            pl.BlockSpec((tile, width), lambda f: (start + f, 0)),
            pl.BlockSpec(memory_space=pl.ANY),
        ]
        + [pl.BlockSpec((BOOKS, tile_groups, unit), lambda f, p=p: (0, start + f, p)) for p in places]
        + [pl.BlockSpec((1, unit), lambda f, p=p: (0, p)) for p in places]
        + [pl.BlockSpec(p.shape, lambda f: (0, 0), pipeline_mode=once) for p in pieces],
        out_specs=out_specs,
        out_shape=out_shape,
        scratch_shapes=[pltpu.VMEM((BOOKS, LOW * 8 * GROUP, 8 * HIGH), jnp.float32)],
        compiler_params=pltpu.CompilerParams(vmem_limit_bytes=VMEM),
        cost_estimate=pl.CostEstimate(
            flops=9 * tokens * features * width * (end - start) // tiles,
            bytes_accessed=2 * (tokens + 2 * features) * width * (end - start) // tiles,
            transcendentals=0,
        ),
        name="weight_gradients",
    )(me, x, weights, after, *([codes] * parts), *([coef] * parts), *pieces)
    return result if len(pieces) > 1 else [pieces[0], *result]


def input_gradient_kernel(count, refs):
    left = jnp.concatenate([refs[s][...] for s in range(count)], axis=1)
    right = jnp.concatenate([refs[count + s][...] for s in range(count)], axis=1)
    return lax.dot_general(left, right, (((1,), (1,)), ((), ())), preferred_element_type=jnp.float32)


def early_kernel(count, added, *refs):
    total = input_gradient_kernel(count, refs)
    total = refs[2 * count][...].astype(jnp.float32) + total if added else total
    refs[-1][...] = total.astype(refs[-1].dtype)


def early_input_gradient(cots, weights, total, after, dtype=jnp.float32):
    tokens, features = cots[0].shape[0], weights[0].shape[0]
    tile_t, tile_f = largest_tile(tokens, 512), largest_tile(features, 1024)
    width = sum(c.shape[1] for c in cots)
    out_spec = pl.BlockSpec((tile_t, tile_f), lambda f, t: (t, f))
    args = [*cots, *weights] + ([] if total is None else [total]) + [after]
    return pl.pallas_call(
        functools.partial(early_kernel, len(cots), total is not None),
        grid=(features // tile_f, tokens // tile_t),
        in_specs=[pl.BlockSpec((tile_t, c.shape[1]), lambda f, t: (t, 0)) for c in cots]
        + [pl.BlockSpec((tile_f, w.shape[1]), lambda f, t: (f, 0)) for w in weights]
        + ([] if total is None else [out_spec])
        + [pl.BlockSpec(memory_space=pl.ANY)],
        out_specs=out_spec,
        out_shape=jax.ShapeDtypeStruct((tokens, features), dtype),
        input_output_aliases={} if total is None else {2 * len(cots): 0},
        compiler_params=pltpu.CompilerParams(vmem_limit_bytes=VMEM),
        cost_estimate=pl.CostEstimate(
            flops=3 * tokens * features * width,
            bytes_accessed=4 * tokens * features + 2 * (tokens + features) * width,
            transcendentals=0,
        ),
        name="early_input_gradient",
    )(*args)


def last_kernel(n, rows, count, me_ref, early_ref, weight_ref, *refs):
    pieces, (one_ref, two_ref, cot_ref) = refs[:count], refs[count:]
    step, half = pl.program_id(0), pl.num_programs(0) // 2
    width = cot_ref.shape[1]

    @pl.when(step == 0)
    def _():
        for piece, (shift, _, _) in zip(pieces, [(0, 0, rows)] + piece_places(n, rows)):
            chunk = lax.rem(me_ref[0] + shift + 2 * n, n)
            start = pl.multiple_of(chunk * (rows // 2), 16)
            cot_ref[pl.ds(start, rows // 2), :] = piece[...].reshape(rows // 2, width)

    part = lax.dot_general(cot_ref[...], weight_ref[...], (((1,), (1,)), ((), ())), preferred_element_type=jnp.float32)
    total = (early_ref[...].reshape(part.shape).astype(jnp.float32) + part).astype(one_ref.dtype)

    @pl.when(step < half)
    def _():
        one_ref[...] = total

    @pl.when(step >= half)
    def _():
        two_ref[...] = total


def last_input_gradient(me, n, block, pieces, weights, early, dtype):
    rows, width = pieces[0].shape
    tokens, features = early.shape
    once = pl.Buffered(1)
    tile = largest_tile(features // 2, 512)
    half = features // 2 // tile
    pairs = rows // (2 * block)
    return pl.pallas_call(
        functools.partial(last_kernel, n, rows, len(pieces)),
        grid_spec=pltpu.PrefetchScalarGridSpec(
            num_scalar_prefetch=1,
            grid=(2 * half,),
            in_specs=[
                pl.BlockSpec((tokens // (2 * block), 1, block, tile), lambda f, who: (0, who[1], 0, f)),
                pl.BlockSpec((tile, width), lambda f, who: (f, 0)),
            ]
            + [pl.BlockSpec((pairs, 1, block, width), lambda f, who: (0, who[1], 0, 0), pipeline_mode=once) for _ in pieces],
            out_specs=[
                pl.BlockSpec((tokens // 2, tile), lambda f, who: (0, jnp.minimum(f, half - 1))),
                pl.BlockSpec((tokens // 2, tile), lambda f, who: (0, jnp.maximum(f - half, 0))),
            ],
            scratch_shapes=[pltpu.VMEM((tokens // 2, width), jnp.bfloat16)],
        ),
        out_shape=[jax.ShapeDtypeStruct((tokens // 2, features // 2), dtype)] * 2,
        compiler_params=pltpu.CompilerParams(vmem_limit_bytes=VMEM),
        cost_estimate=pl.CostEstimate(
            flops=2 * tokens * features * width, bytes_accessed=3 * tokens * features, transcendentals=0
        ),
        name="last_input_gradient",
    )(
        me,
        early.reshape(tokens // (2 * block), 2, block, features),
        weights,
        *[piece.reshape(pairs, 2, block, width) for piece in pieces],
    )


class HalvingScatter:
    def __init__(self, terms, size):
        self.size = size
        self.me = lax.axis_index("dout")
        self.order = list(range(1, size.bit_length() - 1))
        self.step = 0
        rows = 2 * terms[0][0].shape[0] // size
        shape = (2,) * len(self.order) + (rows, terms[0][0].shape[1])
        self.terms = [[t.reshape(shape) for t in half] for half in terms]

    @staticmethod
    def total(terms):
        return sum((t.astype(jnp.float32) for t in terms[1:]), terms[0].astype(jnp.float32))

    def exchange(self, gate=None):
        gives, helds = [], []
        for which in range(2):
            axis, bit = self.place(which)
            mine = (self.me >> bit) & 1
            terms = self.terms[which]
            helds.append([lax.dynamic_index_in_dim(t, mine, axis, keepdims=False) for t in terms])
            give = self.total([lax.dynamic_index_in_dim(t, 1 - mine, axis, keepdims=False) for t in terms])
            gives.append(give.astype(jnp.bfloat16))
        if gate is not None:
            gives, gate = lax.optimization_barrier((gives, gate))
        for which in range(2):
            bit = self.place(which)[1]
            came = lax.ppermute(gives[which], "dout", [(a, a ^ (1 << bit)) for a in range(self.size)])
            self.terms[which] = helds[which] + [came]
        self.step += 1
        return gives if gate is None else gate

    def place(self, which):
        order = self.order if which == 0 else self.order[::-1]
        left = [b for b in reversed(self.order) if b not in order[: self.step]]
        return left.index(order[self.step]), order[self.step]

    def hold(self, gate):
        came, gate = lax.optimization_barrier(([terms[-1] for terms in self.terms], gate))
        self.terms = [[*terms[:-1], new] for terms, new in zip(self.terms, came)]
        return gate

    def finish(self):
        return jnp.concatenate([self.total(t) for t in self.terms], axis=-1).astype(jnp.bfloat16)


def butterfly_sum(value, axis, size):
    if size & (size - 1):
        return lax.psum(value, axis)

    def other(bits):
        return lax.ppermute(value, axis, [(a, a ^ bits) for a in range(size)])

    bit = 1
    while bit < size:
        if 2 * bit < size:
            near, far, both = other(bit), other(2 * bit), other(3 * bit)
            value = (value + near) + (far + both)
            bit *= 4
        else:
            value = value + other(bit)
            bit *= 2
    return value


def local(n_din, n_dout, inputs, cotangent, codes, codebooks, scales, book_mean, book_var, scale_mean, scale_var):
    norm_factor = 1.0 / (2.0 * DOUT) ** 0.5
    loss_scale = (TOKENS * DIN / 4096.0) ** 0.5
    coef = scales * norm_factor
    outs = codes.shape[2]
    me = lax.axis_index("din").astype(jnp.int32).reshape(1)

    table, unit = packed_table(codebooks)
    coef_row = coef.reshape(1, outs)
    unit_row = coef_row * unit

    widths = split_columns(outs)
    firsts = [sum(widths[:i]) for i in range(len(widths))]
    final = len(widths) - 1
    owns = [lax.slice_in_dim(cotangent, f, f + w, axis=1) for f, w in zip(firsts, widths)]
    rings = [Ring(n_din, own.shape[0]) for own in owns]
    weights = [None] * len(widths)
    books, scale_parts, cots = [], [], []

    def run_decode(s, after):
        weights[s] = decode(codes, table, unit_row, after, firsts[s], widths[s])

    def run_gradients(s, after, span=(0, 1)):
        pieces = rings[s].pieces if span[0] == 0 else [cots[s]]
        cot, book, scale = gradients(
            me, n_din, codes, x, pieces, weights[s], coef_row, after, firsts[s], widths[s], span
        )
        if span[0] == 0:
            cots.append(cot)
            scale_parts.append(jnp.sum(scale, axis=0))
        else:
            scale_parts[s] += jnp.sum(scale, axis=0)
        books.append(book)
        return scale

    blocks, owns[0] = lax.optimization_barrier((inputs, owns[0]))
    if inputs.shape[0] % LANES == 0:
        x = lax.all_gather(transpose(blocks), "dout", axis=0, tiled=True)
        x = x.reshape(n_dout, inputs.shape[1], inputs.shape[0])
    else:
        x = lax.all_gather(blocks, "dout", axis=0, tiled=True).T[None]
    rings[0].begin(owns[0])
    run_decode(0, coef_row)
    if final > 0:
        run_decode(1, coef_row)
    early, summed, gate = None, 0, weights[min(1, final)]
    for s in range(final + 1):
        gate = rings[s].hold(gate)
        if s == 0:
            weights[min(1, final)] = gate
        rings[s].finish()
        if s == 0 and final >= 2:
            run_decode(2, gate)
            gate = weights[2]
        if 0 < s < final + 1:
            early = early_input_gradient(cots[summed:], weights[summed:s], early, gate, jnp.bfloat16)
            summed, gate = s, early
        if s < final:
            gate = rings[s].hold(gate)
            owns[s + 1], gate = lax.optimization_barrier((owns[s + 1], gate))
            if s > 0:
                early = gate
            elif final >= 2:
                weights[2] = gate
            rings[s + 1].begin(owns[s + 1])
            gate = run_gradients(s, gate)
            if s == 0:
                for later in range(3, final + 1):
                    run_decode(later, gate)
                    gate = weights[later]

    block = inputs.shape[0]
    if early is not None and n_dout > 1 and n_dout & (n_dout - 1) == 0 and owns[0].shape[0] % (2 * block) == 0:
        core = lax.axis_index("dout").astype(jnp.int32) & 1
        both_me = [jnp.stack([me[0], 1 - core]), jnp.stack([me[0], core])]
        pieces = rings[final].pieces
        rest = (n_din, block, pieces, weights[final], early)
        give = last_input_gradient(both_me[0], *rest, jnp.bfloat16)
        got = [lax.ppermute(half, "dout", [(a, a ^ 1) for a in range(n_dout)]) for half in give]
        keep = last_input_gradient(both_me[1], *rest, jnp.float32)
        scatter = HalvingScatter([[k, g] for k, g in zip(keep, got)], n_dout)
        gate = keep[0]
        if n_dout > 2:
            gate = lax.optimization_barrier(scatter.exchange())[0]
        cut = 5 / 8 if codes.shape[1] >= 256 else 1
        gate = run_gradients(final, gate, (0, cut))
        while scatter.step < len(scatter.order):
            gate = scatter.exchange(gate)
        if cut < 1:
            run_gradients(final, gate, (cut, 1))
            books[-1] = scatter.hold(books[-1])
        grad_input = scatter.finish()
    else:
        run_gradients(final, gate)
        rows = early_input_gradient(cots, weights, None, gate)
        grad_input = lax.psum_scatter(rows, "dout", scatter_dimension=0, tiled=True).astype(jnp.bfloat16)

    book = sum(books[1:], books[0]).reshape(BOOKS, LOW, GROUP, 8, HIGH).sum(axis=3)
    book = book.transpose(0, 3, 1, 2).reshape(BOOKS * KCODE * GROUP)
    scale_total = jnp.concatenate(scale_parts) / coef
    both = butterfly_sum(jnp.concatenate([book, scale_total]), "din", n_din)
    grad_sums = butterfly_sum(both[: book.shape[0]], "dout", n_dout).reshape(BOOKS, KCODE, GROUP)
    scale_sums = both[book.shape[0] :]

    book_grad = grad_sums / loss_scale
    scale_grad = scale_sums * norm_factor / loss_scale
    new_books, new_book_mean, new_book_var = adam_step(codebooks, book_mean, book_var, book_grad)
    new_scales, new_scale_mean, new_scale_var = adam_step(scales, scale_mean, scale_var, scale_grad)
    return (
        grad_input,
        book_grad,
        new_books,
        new_book_mean,
        new_book_var,
        new_scales,
        new_scale_mean,
        new_scale_var,
    )


def solution(mesh):
    in_specs = (
        P("dout", "din"),
        P("din", "dout"),
        P(None, "din", "dout"),
        P(),
        P("dout"),
        P(),
        P(),
        P("dout"),
        P("dout"),
    )
    out_specs = (P("dout", "din"), P(), P(), P(), P(), P("dout"), P("dout"), P("dout"))
    body = functools.partial(local, mesh.shape["din"], mesh.shape["dout"])
    return jax.shard_map(body, mesh=mesh, in_specs=in_specs, out_specs=out_specs, check_vma=False)
```
